128 devices in a mesh: dp: 4 (over x), block: 32 (over z, y, core).
Axes of the slice: x: 4, y: 4, z: 4, core: 2. Of those that a mesh axis runs over, the one named last changes fastest.
Arguments:
- grad: float32 [1024, 28672], P(('dp', 'block')), may hold values from -6 to 6
- factors: float32 [4, 32, 1024, 1024], P('dp', 'block'), as said below
- owners: int32 [28], replicated, may hold values from 0 to 31, as said below
Outputs:
- new_factors: float32 [4, 32, 1024, 1024], P('dp', 'block')
- update: float32 [1024, 28672], P(('dp', 'block'))
The draws below stay inside these ranges and needn't reach their ends.
Inputs may be any that keep to these rules, and one draw needn't show every extreme that they name: `owners`: no owner is named more than 2 times, and some owner exactly 2 times. `factors`: every [1024, 1024] matrix is symmetric positive definite.
All inputs are finite; a program needn't handle non-finite values.
Results may differ from the reference program's by a relative error of at most 0.00013.
Values sent between devices are 32-bit elements; how exact they have to be, the bound alone decides.
No kernel may reach another device: no remote copies, remote signals or barrier semaphores. Data moves between devices by JAX's collectives and lax.ppermute only.
A program may use at most 128 MiB of HBM per device.

```python
import jax
import jax.numpy as jnp
import numpy as np
from jax import lax

BS = 1024
SLOTS = 2
NEWTON = 2
OWNERS = 32
COLB = 28


def draw_owners(key, part):
    key = jax.random.fold_in(key, 2)
    first_key, second_key = jax.random.split(key)
    shuffled = jax.random.permutation(first_key, OWNERS)
    doubled = COLB // 4
    base_table = np.array([c // 2 if c < 2 * doubled else c - doubled for c in range(COLB)], dtype=np.int32)
    listed = shuffled[base_table]
    ordering = jax.random.permutation(second_key, COLB)
    return listed[ordering].astype(jnp.int32)


def draw_factors(key, part):
    key = jax.random.fold_in(key, 1)
    scale_key, entry_key = jax.random.split(key)
    low_end, high_end, ridge = (0.7, 1.42, 0.15)
    identity = jnp.eye(BS, dtype=jnp.float32)

    def one_matrix(index):
        sub_key = jax.random.fold_in(entry_key, index)
        noise = jax.random.normal(sub_key, (BS, BS), jnp.float32)
        gram = jnp.dot(noise, noise.T, precision=lax.Precision.HIGHEST) / BS
        return 0.5 * (gram + gram.T) + ridge * identity
    count = 2 * SLOTS * OWNERS
    grams = lax.map(one_matrix, jnp.arange(count, dtype=jnp.int32)).reshape(2 * SLOTS, OWNERS, BS, BS)
    log_scales = jax.random.uniform(scale_key, (2 * SLOTS, OWNERS, BS), jnp.float32, jnp.log(low_end), jnp.log(high_end))
    row_scales = jnp.exp(log_scales)
    return row_scales[..., :, None] * row_scales[..., None, :] * grams


def block_scale(own_key, extent, cuts, smallest, high):
    def one(dim, shards_of):
        draws = jax.random.uniform(jax.random.fold_in(jax.random.fold_in(own_key, 6), dim), (shards_of,), jnp.float32, smallest / len(cuts), high / len(cuts))
        return jnp.repeat(jnp.exp(draws), extent[dim] // shards_of).reshape((-1,) + (1,) * (len(extent) - dim - 1))

    loudness = one(*cuts[0])
    for cut in cuts[1:]:
        loudness = loudness * one(*cut)
    return loudness


def scatter_about(key, dims, spread, reach, cuts=(), held_as=jnp.bfloat16):
    gain = block_scale(key, dims, cuts, -0.22, 0.18) if cuts else 1.0
    values = jax.random.normal(key, dims, jnp.float32) * spread * gain
    return jnp.minimum(jnp.maximum(values, -reach), reach).astype(held_as)


def setup_inputs(seed: int = 0) -> dict:
    splits = jax.random.split(jax.random.key(seed), 4)
    return {
        "grad": scatter_about(splits[0], (BS, COLB * BS), 1.0, 6.0, ((0, 128),), jnp.float32),
        "factors": draw_factors(jax.random.fold_in(splits[3], 71), 0),
        "owners": draw_owners(jax.random.fold_in(splits[3], 71), 0),
    }


precise = lax.Precision.HIGHEST
decay_rate = 0.9
epsilon = 1e-06

def inverse_root(matrix):
    order_size = matrix.shape[0]
    identity = jnp.eye(order_size, dtype=jnp.float32)
    trace_scale = 2.0 * jnp.trace(matrix) / order_size
    coupled = matrix / trace_scale
    result = identity
    for iteration in range(NEWTON):
        factor_step = (5.0 * identity - coupled) * 0.25
        if iteration == 0:
            result = factor_step
        else:
            result = jnp.dot(result, factor_step, precision=precise)
        if iteration + 1 < NEWTON:
            squared = jnp.dot(factor_step, factor_step, precision=precise)
            coupled = jnp.dot(jnp.dot(squared, squared, precision=precise), coupled, precision=precise)
    return result

def slot_numbers(owners):
    count = owners.shape[0]
    same_owner = owners[:, None] == owners[None, :]
    earlier = jnp.arange(count)[None, :] < jnp.arange(count)[:, None]
    return lax.optimization_barrier(jnp.sum(same_owner & earlier, axis=1)).astype(jnp.int32)

def reference(grad, factors, owners):
    col_blocks = owners.shape[0]
    slots = slot_numbers(owners)
    blocks = grad.reshape(BS, col_blocks, BS).transpose(1, 0, 2)

    def per_block(items):
        block_grad, owner_id, slot_id = items
        left_root = inverse_root(factors[2 * slot_id, owner_id])
        right_root = inverse_root(factors[2 * slot_id + 1, owner_id])
        raw = jnp.dot(jnp.dot(left_root, block_grad, precision=precise), right_root, precision=precise)
        grad_mean = jnp.mean(block_grad * block_grad)
        raw_mean = jnp.mean(raw * raw)
        grafted = raw * (jnp.sqrt(grad_mean + epsilon) / jnp.sqrt(raw_mean + epsilon))
        left_term = (1.0 - decay_rate) / BS * jnp.dot(block_grad, block_grad.T, precision=precise)
        right_term = (1.0 - decay_rate) / BS * jnp.dot(block_grad.T, block_grad, precision=precise)
        return (grafted, left_term, right_term)
    grafted, left_terms, right_terms = lax.map(per_block, (blocks, owners, slots))
    new_factors = decay_rate * factors
    new_factors = new_factors.at[2 * slots, owners].add(left_terms)
    new_factors = new_factors.at[2 * slots + 1, owners].add(right_terms)
    update = grafted.transpose(1, 0, 2).reshape(BS, col_blocks * BS)
    return (new_factors, update)
```

```python
import jax
import jax.numpy as jnp
from jax import lax
from jax.experimental import pallas as pl
from jax.experimental.pallas import tpu as pltpu
from jax.sharding import PartitionSpec as P

BOTH = ("dp", "block")
TILE = 256
VMEM_LIMIT = 56 * 1024 * 1024

decay_rate = 0.9
epsilon = 1e-06


def vmem():
    return pl.BlockSpec(memory_space=pltpu.VMEM)


def smem():
    return pl.BlockSpec(memory_space=pltpu.SMEM)


def diag_mask():
    rows = lax.broadcasted_iota(jnp.int32, (TILE, TILE), 0)
    cols = lax.broadcasted_iota(jnp.int32, (TILE, TILE), 1)
    return rows, cols


def span(index):
    return slice(index * TILE, (index + 1) * TILE)


def split(value):
    high = value.astype(jnp.bfloat16)
    low = (value - high.astype(jnp.float32)).astype(jnp.bfloat16)
    return high, low


def dot3(a_high, a_low, b_high, b_low):
    def one(a, b):
        return jnp.dot(a, b, preferred_element_type=jnp.float32)

    return one(a_high, b_high) + (one(a_high, b_low) + one(a_low, b_high))


def put_split(high_ref, low_ref, i, j, block):
    high, low = split(block)
    high_ref[span(i), span(j)] = high
    low_ref[span(i), span(j)] = low


def put_both(high_ref, low_ref, i, j, block):
    put_split(high_ref, low_ref, i, j, block)
    if i != j:
        put_split(high_ref, low_ref, j, i, block.T)


def deal_kernel(owners_ref, grad_ref, out_ref, count_ref):
    owner_count = count_ref.shape[0]
    col_blocks = owners_ref.shape[0]
    width = out_ref.shape[-1]

    @pl.loop(0, owner_count)
    def _(o):
        count_ref[o] = 0

    out_ref[...] = jnp.zeros_like(out_ref)

    @pl.loop(0, col_blocks)
    def _(c):
        owner = owners_ref[c]
        slot = count_ref[owner]
        count_ref[owner] = slot + 1
        cols = pl.ds(pl.multiple_of(c * width, width), width)
        out_ref[slot * owner_count + owner] = grad_ref[:, cols]


def deal(owners, grad, owner_count):
    rows = grad.shape[0]
    width = grad.shape[1] // owners.shape[0]
    return pl.pallas_call(
        deal_kernel,
        out_shape=jax.ShapeDtypeStruct((2 * owner_count, rows, width), jnp.float32),
        in_specs=[smem(), vmem()],
        out_specs=vmem(),
        scratch_shapes=[pltpu.SMEM((owner_count,), jnp.int32)],
        compiler_params=pltpu.CompilerParams(vmem_limit_bytes=VMEM_LIMIT),
        cost_estimate=pl.CostEstimate(flops=0, bytes_accessed=3 * 2**20, transcendentals=0),
        name="deal",
    )(owners, grad)


def collect_kernel(owners_ref, scale_ref, back_ref, out_ref, count_ref):
    owner_count = count_ref.shape[0]
    col_blocks = owners_ref.shape[0]
    width = back_ref.shape[-1]

    @pl.loop(0, owner_count)
    def _(o):
        count_ref[o] = 0

    @pl.loop(0, col_blocks)
    def _(c):
        owner = owners_ref[c]
        slot = count_ref[owner]
        count_ref[owner] = slot + 1
        place = slot * owner_count + owner
        cols = pl.ds(pl.multiple_of(c * width, width), width)
        out_ref[:, cols] = back_ref[place] * scale_ref[place]


def collect(owners, scales, back):
    places, rows, width = back.shape
    return pl.pallas_call(
        collect_kernel,
        out_shape=jax.ShapeDtypeStruct((rows, owners.shape[0] * width), jnp.float32),
        in_specs=[smem(), smem(), vmem()],
        out_specs=vmem(),
        scratch_shapes=[pltpu.SMEM((places // 2,), jnp.int32)],
        compiler_params=pltpu.CompilerParams(vmem_limit_bytes=VMEM_LIMIT),
        cost_estimate=pl.CostEstimate(flops=0, bytes_accessed=3 * 2**20, transcendentals=0),
        name="collect",
    )(owners, scales, back)


def lower_blocks(tiles):
    return [(i, j) for j in range(tiles) for i in range(j + 1, tiles)]


def root_kernel(a_ref, xh_ref, xl_ref, pack_ref, sh, sl, s2, s2h, s2l, s3h, s3l, qh, ql):
    size = a_ref.shape[0]
    tiles = size // TILE
    rows, cols = diag_mask()
    on_diag = rows == cols
    trace = jnp.float32(0.0)
    for b in range(tiles):
        trace += jnp.sum(jnp.where(on_diag, a_ref[span(b), span(b)], 0.0))
    shrink = 0.25 / (2.0 * trace / size)

    def step_block(i, j):
        block = a_ref[span(i), span(j)] * -shrink
        if i == j:
            block = jnp.where(on_diag, 1.25 + block, block)
        return block

    for i in range(tiles):
        for j in range(tiles):
            put_split(sh, sl, i, j, step_block(i, j))

    def product(ah, al, bh, bl, j):
        low_rows = slice(j * TILE, size)
        return dot3(ah[low_rows, :], al[low_rows, :], bh[:, span(j)], bl[:, span(j)])

    for j in range(tiles):
        column = product(sh, sl, sh, sl, j)
        s2[j * TILE :, span(j)] = column
        for i in range(j, tiles):
            put_both(s2h, s2l, i, j, column[span(i - j)])
    for j in range(tiles):
        column = product(sh, sl, s2h, s2l, j)
        for i in range(j, tiles):
            block = column[span(i - j)]
            put_both(s3h, s3l, i, j, block)
            put_both(qh, ql, i, j, block - 1.25 * s2[span(i), span(j)])
    for j in range(tiles):
        column = product(s3h, s3l, qh, ql, j)
        for i in range(j, tiles):
            block = column[span(i - j)] + 1.25 * step_block(i, j)
            put_both(xh_ref, xl_ref, i, j, block)
            if i != j:
                pack_ref[span(lower_blocks(tiles).index((i, j)))] = block
            else:
                s2[span(i), span(i)] = block
    offset = len(lower_blocks(tiles))
    last = (offset + tiles // 2) * TILE
    for pair in range(tiles // 2):
        first = s2[span(2 * pair), span(2 * pair)]
        second = s2[span(2 * pair + 1), span(2 * pair + 1)]
        pack_ref[span(offset + pair)] = jnp.where(rows >= cols, first, second)
        diagonal = jnp.sum(jnp.where(on_diag, second, 0.0), axis=0, keepdims=True)
        pack_ref[last + pair * 8 : last + pair * 8 + 8] = jnp.broadcast_to(diagonal, (8, TILE))


def packed_rows(size):
    tiles = size // TILE
    return (len(lower_blocks(tiles)) + tiles // 2) * TILE + 8 * (tiles // 2)


def root(factor):
    size = factor.shape[0]
    half = jax.ShapeDtypeStruct((size, size), jnp.bfloat16)
    return pl.pallas_call(
        root_kernel,
        out_shape=[half, half, jax.ShapeDtypeStruct((packed_rows(size), TILE), jnp.float32)],
        in_specs=[vmem()],
        out_specs=[vmem()] * 3,
        scratch_shapes=[pltpu.VMEM((size, size), jnp.bfloat16)] * 2
        + [pltpu.VMEM((size, size), jnp.float32)]
        + [pltpu.VMEM((size, size), jnp.bfloat16)] * 6,
        compiler_params=pltpu.CompilerParams(vmem_limit_bytes=VMEM_LIMIT),
        cost_estimate=pl.CostEstimate(
            flops=11 * size**3, bytes_accessed=10 * 2**20, transcendentals=0
        ),
        name="root",
    )(factor)


def unpack_block(pack_ref, tiles, i, j, rows, cols):
    if i != j:
        return pack_ref[span(lower_blocks(tiles).index((i, j)))]
    offset = len(lower_blocks(tiles))
    last = (offset + tiles // 2) * TILE
    both = pack_ref[span(offset + i // 2)]
    if i % 2 == 0:
        return jnp.where(rows >= cols, both, both.T)
    diagonal = pack_ref[last + (i // 2) * 8 : last + (i // 2) * 8 + 1]
    return jnp.where(rows == cols, diagonal, jnp.where(rows < cols, both, both.T))


def apply_kernel(
    place_ref, xh_ref, xl_ref, pack_ref, near_ref, far_ref, raw_ref, sums_ref,
    ph, pw, lh, ll, rh, rl, gh, gl, uh, ul,
):
    size = xh_ref.shape[0]
    half = size // 2
    tiles = size // TILE
    side = place_ref[0]
    rows, cols = diag_mask()

    for i in range(tiles):
        for j in range(i + 1):
            put_both(ph, pw, i, j, unpack_block(pack_ref, tiles, i, j, rows, cols))

    def place_left(high_ref, low_ref):
        for r in range(2):
            source_rows = pl.ds(pl.multiple_of(place_ref[1 + r] * TILE, TILE), TILE)
            for c in range(tiles):
                source_cols = pl.ds(pl.multiple_of(place_ref[1 + c] * TILE, TILE), TILE)
                lh[span(r), span(c)] = high_ref[source_rows, source_cols]
                ll[span(r), span(c)] = low_ref[source_rows, source_cols]

    @pl.when(side == 0)
    def _():
        place_left(xh_ref, xl_ref)
        rh[...] = ph[...]
        rl[...] = pw[...]

    @pl.when(side != 0)
    def _():
        place_left(ph, pw)
        rh[...] = xh_ref[...]
        rl[...] = xl_ref[...]

    total = jnp.zeros((8, TILE), jnp.float32)
    for part, ref in enumerate((near_ref, far_ref)):
        for r in range(half // TILE):
            for c in range(tiles):
                block = ref[span(r), span(c)]
                put_split(gh, gl, part * (half // TILE) + r, c, block)
                total += jnp.sum((block * block).reshape(TILE // 8, 8, TILE), axis=0)
    grad_sum = jnp.sum(total)
    for j in range(tiles):
        column = dot3(lh[...], ll[...], gh[:, span(j)], gl[:, span(j)])
        high, low = split(column)
        uh[:, span(j)] = high
        ul[:, span(j)] = low
    total = jnp.zeros((8, TILE), jnp.float32)
    for j in range(tiles):
        column = dot3(uh[...], ul[...], rh[:, span(j)], rl[:, span(j)])
        raw_ref[:, span(j)] = column
        total += jnp.sum((column * column).reshape(half // 8, 8, TILE), axis=0)
    raw_sum = jnp.sum(total)
    lane = lax.broadcasted_iota(jnp.int32, (8, 128), 1)
    sums_ref[...] = jnp.where(lane == 0, raw_sum, jnp.where(lane == 1, grad_sum, 0.0))


def apply_roots(place, x_high, x_low, pack, near, far):
    size = x_high.shape[0]
    half = size // 2
    big = pltpu.VMEM((size, size), jnp.bfloat16)
    small = pltpu.VMEM((half, size), jnp.bfloat16)
    return pl.pallas_call(
        apply_kernel,
        out_shape=[
            jax.ShapeDtypeStruct((half, size), jnp.float32),
            jax.ShapeDtypeStruct((8, 128), jnp.float32),
        ],
        in_specs=[smem()] + [vmem()] * 5,
        out_specs=[vmem()] * 2,
        scratch_shapes=[big, big, small, small, big, big, big, big, small, small],
        compiler_params=pltpu.CompilerParams(vmem_limit_bytes=VMEM_LIMIT),
        cost_estimate=pl.CostEstimate(
            flops=6 * size**3, bytes_accessed=12 * 2**20, transcendentals=0
        ),
        name="apply_roots",
    )(place, x_high, x_low, pack, near, far)


def per_device(grad, factors, owners):
    row_count = grad.shape[0]
    block_size = factors.shape[-1]
    owner_count = lax.axis_size("block")
    dp_index = lax.axis_index("dp")
    blk_index = lax.axis_index("block")
    side = dp_index % 2
    slot = dp_index // 2
    outer_pair = (dp_index == 0) | (dp_index == 3)
    groups = [[x * owner_count + b for x in pair for b in range(owner_count)] for pair in ((0, 3), (1, 2))]

    def exchange(x):
        return lax.all_to_all(
            x, BOTH, split_axis=0, concat_axis=0, tiled=True, axis_index_groups=groups
        )

    def swap(x):
        return lax.ppermute(x, "dp", [(i, i ^ 1) for i in range(4)])

    other_grad = swap(grad)
    near = exchange(deal(owners, grad, owner_count)).reshape(block_size // 2, block_size)
    own_factor = factors[0, 0]
    x_high, x_low, pack = root(own_factor)
    pack, other_grad = lax.optimization_barrier((pack, other_grad))
    other_pack = swap(pack)
    far = exchange(deal(owners, other_grad, owner_count)).reshape(block_size // 2, block_size)

    order = jnp.where(outer_pair, jnp.array([0, 3, 1, 2]), jnp.array([1, 2, 0, 3]))
    place = jnp.concatenate([side[None], order]).astype(jnp.int32)
    raw, sums = apply_roots(place, x_high, x_low, other_pack, near, far)
    back = exchange(raw.reshape(2 * owner_count, row_count, block_size))
    all_sums = lax.all_gather(sums[0], BOTH)
    raw_sums = all_sums[:, 0].reshape(2, 2, owner_count).sum(axis=1).reshape(-1)
    grad_sums = all_sums[:, 1].reshape(2, 2, owner_count)[:, 0].reshape(-1)
    count = block_size * block_size
    scales = jnp.sqrt(grad_sums / count + epsilon) / jnp.sqrt(raw_sums / count + epsilon)
    update = collect(owners, scales, back)

    quarter = block_size // 4
    block_grad = jnp.where(
        outer_pair,
        jnp.concatenate([near[:quarter], far, near[quarter:]]),
        jnp.concatenate([far[:quarter], near, far[quarter:]]),
    )
    flipped = jnp.where(side == 0, block_grad, block_grad.T)
    outer = lax.dot_general(
        flipped, flipped, (((1,), (1,)), ((), ())), precision=lax.Precision.HIGH
    )
    used = jnp.sum(owners == blk_index) > slot
    new_own = decay_rate * own_factor + jnp.where(
        used, (1.0 - decay_rate) / block_size * outer, 0.0
    )
    return (new_own[None, None], update)


def solution(mesh):
    placed = (P(BOTH, None), P("dp", "block", None, None), P())
    return jax.shard_map(
        per_device,
        mesh=mesh,
        in_specs=placed,
        out_specs=(P("dp", "block", None, None), P(BOTH, None)),
        check_vma=False,
    )
```

```python
import jax
import jax.numpy as jnp
from jax import lax
from jax.experimental import pallas as pl
from jax.experimental.pallas import tpu as pltpu
from jax.sharding import PartitionSpec as P

BOTH = ("dp", "block")
TILE = 256
VMEM_LIMIT = 56 * 1024 * 1024

decay_rate = 0.9
epsilon = 1e-06


def vmem():
    return pl.BlockSpec(memory_space=pltpu.VMEM)


def anywhere():
    return pl.BlockSpec(memory_space=pl.ANY)


def smem():
    return pl.BlockSpec(memory_space=pltpu.SMEM)


def diag_mask():
    rows = lax.broadcasted_iota(jnp.int32, (TILE, TILE), 0)
    cols = lax.broadcasted_iota(jnp.int32, (TILE, TILE), 1)
    return rows, cols


def span(index):
    return slice(index * TILE, (index + 1) * TILE)


def split(value):
    high = value.astype(jnp.bfloat16)
    low = (value - high.astype(jnp.float32)).astype(jnp.bfloat16)
    return high, low


def dot3(a_high, a_low, b_high, b_low):
    def one(a, b):
        return jnp.dot(a, b, preferred_element_type=jnp.float32)

    return one(a_high, b_high) + (one(a_high, b_low) + one(a_low, b_high))


def put_split(high_ref, low_ref, i, j, block):
    high, low = split(block)
    high_ref[span(i), span(j)] = high
    low_ref[span(i), span(j)] = low


def put_both(high_ref, low_ref, i, j, block):
    put_split(high_ref, low_ref, i, j, block)
    if i != j:
        put_split(high_ref, low_ref, j, i, block.T)


def place_of(owners_ref, count_ref, c):
    owner = owners_ref[c]
    slot = count_ref[owner]
    count_ref[owner] = slot + 1
    return slot * count_ref.shape[0] + owner


def clear(count_ref):
    @pl.loop(0, count_ref.shape[0])
    def _(o):
        count_ref[o] = 0


def column_copies(count, width, source, target, sems):
    each = -(-count // sems.shape[0])
    copies = []
    for k, first in enumerate(range(0, count, each)):
        cols = slice(first * width, min(first + each, count) * width)
        copies.append(pltpu.make_async_copy(source.at[:, cols], target.at[:, cols], sems.at[k]))
    return each, copies


def deal_kernel(owners_ref, grad_hbm, out_hbm, count_ref, buffer, sems, whole_sems):
    width = out_hbm.shape[-1]
    count = owners_ref.shape[0]
    each, loads = column_copies(count, width, grad_hbm, buffer, whole_sems)
    for load in loads:
        load.start()
    clear(count_ref)
    stores = []
    for c in range(count):
        place = place_of(owners_ref, count_ref, c)
        if c % each == 0:
            loads[c // each].wait()
        cols = slice(c * width, (c + 1) * width)
        stores.append(pltpu.make_async_copy(buffer.at[:, cols], out_hbm.at[place], sems.at[c]))
        stores[-1].start()
    for store in stores:
        store.wait()


def collect_kernel(owners_ref, back_hbm, out_hbm, count_ref, buffer, sems, whole_sems):
    width = back_hbm.shape[-1]
    count = owners_ref.shape[0]
    clear(count_ref)
    loads = []
    for c in range(count):
        place = place_of(owners_ref, count_ref, c)
        cols = slice(c * width, (c + 1) * width)
        loads.append(pltpu.make_async_copy(back_hbm.at[place], buffer.at[:, cols], sems.at[c]))
        loads[-1].start()
    each, stores = column_copies(count, width, buffer, out_hbm, whole_sems)
    for k, store in enumerate(stores):
        for load in loads[k * each : (k + 1) * each]:
            load.wait()
        store.start()
    for store in stores:
        store.wait()


def move_blocks(kernel, name, owners, source, owner_count, shape, flat):
    return pl.pallas_call(
        kernel,
        out_shape=jax.ShapeDtypeStruct(shape, jnp.float32),
        in_specs=[smem(), anywhere()],
        out_specs=anywhere(),
        scratch_shapes=[
            pltpu.SMEM((owner_count,), jnp.int32),
            pltpu.VMEM(flat, jnp.float32),
            pltpu.SemaphoreType.DMA((owners.shape[0],)),
            pltpu.SemaphoreType.DMA((4,)),
        ],
        cost_estimate=pl.CostEstimate(flops=0, bytes_accessed=2 * 2**20, transcendentals=0),
        name=name,
    )(owners, source)


def deal(owners, grad, owner_count):
    rows = grad.shape[0]
    width = grad.shape[1] // owners.shape[0]
    return move_blocks(deal_kernel, "deal", owners, grad, owner_count, (2 * owner_count, rows, width), grad.shape)


def collect(owners, back):
    places, rows, width = back.shape
    shape = (rows, owners.shape[0] * width)
    return move_blocks(collect_kernel, "collect", owners, back, places // 2, shape, shape)


def lower_blocks(tiles):
    return [(i, j) for j in range(tiles) for i in range(j + 1, tiles)]


def root_kernel(a_ref, xh_ref, xl_ref, pack_ref, sh, sl, s2, s2h, s2l, s3h, s3l, qh, ql):
    size = a_ref.shape[0]
    tiles = size // TILE
    rows, cols = diag_mask()
    on_diag = rows == cols
    trace = jnp.float32(0.0)
    for b in range(tiles):
        trace += jnp.sum(jnp.where(on_diag, a_ref[span(b), span(b)], 0.0))
    shrink = 0.25 / (2.0 * trace / size)

    def step_block(i, j):
        block = a_ref[span(i), span(j)] * -shrink
        if i == j:
            block = jnp.where(on_diag, 1.25 + block, block)
        return block

    for i in range(tiles):
        for j in range(tiles):
            put_split(sh, sl, i, j, step_block(i, j))

    def product(ah, al, bh, bl, j):
        low_rows = slice(j * TILE, size)
        return dot3(ah[low_rows, :], al[low_rows, :], bh[:, span(j)], bl[:, span(j)])

    for j in range(tiles):
        column = product(sh, sl, sh, sl, j)
        s2[j * TILE :, span(j)] = column
        for i in range(j, tiles):
            put_both(s2h, s2l, i, j, column[span(i - j)])
    for j in range(tiles):
        column = product(sh, sl, s2h, s2l, j)
        for i in range(j, tiles):
            block = column[span(i - j)]
            put_both(s3h, s3l, i, j, block)
            put_both(qh, ql, i, j, block - 1.25 * s2[span(i), span(j)])
    for j in range(tiles):
        column = product(s3h, s3l, qh, ql, j)
        for i in range(j, tiles):
            block = column[span(i - j)] + 1.25 * step_block(i, j)
            put_both(xh_ref, xl_ref, i, j, block)
            if i != j:
                pack_ref[span(lower_blocks(tiles).index((i, j)))] = block
            else:
                s2[span(i), span(i)] = block
    offset = len(lower_blocks(tiles))
    last = (offset + tiles // 2) * TILE
    for pair in range(tiles // 2):
        first = s2[span(2 * pair), span(2 * pair)]
        second = s2[span(2 * pair + 1), span(2 * pair + 1)]
        pack_ref[span(offset + pair)] = jnp.where(rows >= cols, first, second)
        diagonal = jnp.sum(jnp.where(on_diag, second, 0.0), axis=0, keepdims=True)
        pack_ref[last + pair * 8 : last + pair * 8 + 8] = jnp.broadcast_to(diagonal, (8, TILE))


def packed_rows(size):
    tiles = size // TILE
    return (len(lower_blocks(tiles)) + tiles // 2) * TILE + 8 * (tiles // 2)


def root(factor):
    size = factor.shape[0]
    half = jax.ShapeDtypeStruct((size, size), jnp.bfloat16)
    return pl.pallas_call(
        root_kernel,
        out_shape=[half, half, jax.ShapeDtypeStruct((packed_rows(size), TILE), jnp.float32)],
        in_specs=[vmem()],
        out_specs=[vmem()] * 3,
        scratch_shapes=[pltpu.VMEM((size, size), jnp.bfloat16)] * 2
        + [pltpu.VMEM((size, size), jnp.float32)]
        + [pltpu.VMEM((size, size), jnp.bfloat16)] * 6,
        compiler_params=pltpu.CompilerParams(vmem_limit_bytes=VMEM_LIMIT),
        cost_estimate=pl.CostEstimate(
            flops=0, bytes_accessed=0, transcendentals=0
        ),
        name="root",
    )(factor)


def unpack_block(pack_ref, tiles, i, j, rows, cols):
    if i != j:
        return pack_ref[span(lower_blocks(tiles).index((i, j)))]
    offset = len(lower_blocks(tiles))
    last = (offset + tiles // 2) * TILE
    both = pack_ref[span(offset + i // 2)]
    if i % 2 == 0:
        return jnp.where(rows >= cols, both, both.T)
    diagonal = pack_ref[last + (i // 2) * 8 : last + (i // 2) * 8 + 1]
    return jnp.where(rows == cols, diagonal, jnp.where(rows < cols, both, both.T))


def split_kernel(x_ref, high_ref, low_ref, sum_ref):
    half, size = x_ref.shape
    total = jnp.zeros((8, TILE), jnp.float32)
    for r in range(half // TILE):
        for c in range(size // TILE):
            block = x_ref[span(r), span(c)]
            put_split(high_ref, low_ref, r, c, block)
            total += jnp.sum((block * block).reshape(TILE // 8, 8, TILE), axis=0)
    sum_ref[...] = jnp.full(sum_ref.shape, jnp.sum(total), jnp.float32)


def split_rows(x):
    half = jax.ShapeDtypeStruct(x.shape, jnp.bfloat16)
    return pl.pallas_call(
        split_kernel,
        out_shape=[half, half, jax.ShapeDtypeStruct((8, 128), jnp.float32)],
        in_specs=[vmem()],
        out_specs=[vmem()] * 3,
        compiler_params=pltpu.CompilerParams(vmem_limit_bytes=VMEM_LIMIT),
        cost_estimate=pl.CostEstimate(flops=0, bytes_accessed=4 * 2**20, transcendentals=0),
        name="split_rows",
    )(x)


def near_kernel(
    place_ref, xh_ref, xl_ref, pack_ref, nh_ref, nl_ref, v_ref, fh_ref, fl_ref, rh, rl, ph, pw, lh, ll
):
    size = xh_ref.shape[0]
    tiles = size // TILE
    side = place_ref[0]
    rows, cols = diag_mask()

    def place_left(high_ref, low_ref):
        for r in range(2):
            source_rows = pl.ds(pl.multiple_of(place_ref[1 + r] * TILE, TILE), TILE)
            for c in range(tiles):
                source_cols = pl.ds(pl.multiple_of(place_ref[1 + c] * TILE, TILE), TILE)
                to_high, to_low = (lh, ll) if c < 2 else (fh_ref, fl_ref)
                to_high[span(r), span(c % 2)] = high_ref[source_rows, source_cols]
                to_low[span(r), span(c % 2)] = low_ref[source_rows, source_cols]

    def unpack(high_ref, low_ref):
        for i in range(tiles):
            for j in range(i + 1):
                put_both(high_ref, low_ref, i, j, unpack_block(pack_ref, tiles, i, j, rows, cols))

    @pl.when(side == 0)
    def _():
        place_left(xh_ref, xl_ref)
        unpack(rh, rl)

    @pl.when(side != 0)
    def _():
        unpack(ph, pw)
        place_left(ph, pw)
        rh[...] = xh_ref[...]
        rl[...] = xl_ref[...]

    for j in range(tiles):
        v_ref[:, span(j)] = dot3(lh[...], ll[...], nh_ref[:, span(j)], nl_ref[:, span(j)])


def near_part(place, x_high, x_low, pack, near_high, near_low):
    size = x_high.shape[0]
    half = size // 2
    big = pltpu.VMEM((size, size), jnp.bfloat16)
    small = pltpu.VMEM((half, half), jnp.bfloat16)
    full_out = jax.ShapeDtypeStruct((size, size), jnp.bfloat16)
    quarter_out = jax.ShapeDtypeStruct((half, half), jnp.bfloat16)
    return pl.pallas_call(
        near_kernel,
        out_shape=[
            jax.ShapeDtypeStruct((half, size), jnp.float32),
            quarter_out, quarter_out, full_out, full_out,
        ],
        in_specs=[smem()] + [vmem()] * 5,
        out_specs=[vmem()] * 5,
        scratch_shapes=[big, big, small, small],
        compiler_params=pltpu.CompilerParams(vmem_limit_bytes=VMEM_LIMIT),
        cost_estimate=pl.CostEstimate(
            flops=3 * size**3, bytes_accessed=12 * 2**20, transcendentals=0
        ),
        name="near_part",
    )(place, x_high, x_low, pack, near_high, near_low)


def far_kernel(
    far_hbm, lh_hbm, ll_hbm, v_hbm, rh_hbm, rl_hbm, near_sum_ref, raw_hbm, gh_hbm, gl_hbm, sums_ref,
    far, lh, ll, v, rh, rl, gh, gl, uh, ul, raw, in_sems, out_sems,
):
    half, size = far.shape
    tiles = size // TILE
    sources = (far_hbm, lh_hbm, ll_hbm, v_hbm, rh_hbm, rl_hbm)
    loads = [
        pltpu.make_async_copy(source, target, in_sems.at[k])
        for k, (source, target) in enumerate(zip(sources, (far, lh, ll, v, rh, rl)))
    ]
    for load in loads:
        load.start()
    for load in loads[:4]:
        load.wait()
    total = jnp.zeros((8, TILE), jnp.float32)
    for j in range(tiles):
        block = far[:, span(j)]
        high, low = split(block)
        gh[:, span(j)] = high
        gl[:, span(j)] = low
        total += jnp.sum((block * block).reshape(half // 8, 8, TILE), axis=0)
        column = v[:, span(j)] + dot3(lh[...], ll[...], high, low)
        high, low = split(column)
        uh[:, span(j)] = high
        ul[:, span(j)] = low
    stores = [
        pltpu.make_async_copy(gh, gh_hbm, out_sems.at[tiles]),
        pltpu.make_async_copy(gl, gl_hbm, out_sems.at[tiles + 1]),
    ]
    for store in stores:
        store.start()
    grad_sum = jnp.sum(total) + near_sum_ref[0, 0]
    for load in loads[4:]:
        load.wait()
    total = jnp.zeros((8, TILE), jnp.float32)
    for j in range(tiles):
        column = dot3(uh[...], ul[...], rh[:, span(j)], rl[:, span(j)])
        raw[:, span(j)] = column
        stores.append(
            pltpu.make_async_copy(raw.at[:, span(j)], raw_hbm.at[:, span(j)], out_sems.at[j])
        )
        stores[-1].start()
        total += jnp.sum((column * column).reshape(half // 8, 8, TILE), axis=0)
    raw_sum = jnp.sum(total)
    lane = lax.broadcasted_iota(jnp.int32, (8, 128), 1)
    sums_ref[...] = jnp.where(lane == 0, raw_sum, grad_sum)
    for store in stores:
        store.wait()


def far_part(far, left_high, left_low, v, right_high, right_low, near_sum):
    half, size = far.shape
    tiles = size // TILE
    wide = pltpu.VMEM((half, size), jnp.bfloat16)
    wide_f32 = pltpu.VMEM((half, size), jnp.float32)
    square = pltpu.VMEM((half, half), jnp.bfloat16)
    big = pltpu.VMEM((size, size), jnp.bfloat16)
    wide_out = jax.ShapeDtypeStruct((half, size), jnp.bfloat16)
    return pl.pallas_call(
        far_kernel,
        out_shape=[
            jax.ShapeDtypeStruct((half, size), jnp.float32),
            wide_out,
            wide_out,
            jax.ShapeDtypeStruct((8, 128), jnp.float32),
        ],
        in_specs=[anywhere()] * 6 + [vmem()],
        out_specs=[anywhere()] * 3 + [vmem()],
        scratch_shapes=[
            wide_f32, square, square, wide_f32, big, big, wide, wide, wide, wide, wide_f32,
            pltpu.SemaphoreType.DMA((6,)),
            pltpu.SemaphoreType.DMA((tiles + 2,)),
        ],
        compiler_params=pltpu.CompilerParams(vmem_limit_bytes=VMEM_LIMIT),
        cost_estimate=pl.CostEstimate(
            flops=5 * size**3, bytes_accessed=12 * 2**20, transcendentals=0
        ),
        name="far_part",
    )(far, left_high, left_low, v, right_high, right_low, near_sum)


def graft_kernel(own_ref, other_ref, raw_hbm, out_hbm, buffer, in_sems, out_sems):
    half, size = buffer.shape
    steps = in_sems.shape[0]
    count = size * size
    loads, stores = [], []
    for k in range(steps):
        rows = slice(k * half // steps, (k + 1) * half // steps)
        loads.append(pltpu.make_async_copy(raw_hbm.at[rows], buffer.at[rows], in_sems.at[k]))
        stores.append(pltpu.make_async_copy(buffer.at[rows], out_hbm.at[rows], out_sems.at[k]))
    for load in loads:
        load.start()
    own = own_ref[...]
    raw_sum = own[:1, :1] + other_ref[:1, :1]
    grad_sum = own[:1, 1:2]
    scale = jnp.sqrt(grad_sum / count + epsilon) / jnp.sqrt(raw_sum / count + epsilon)
    for k in range(steps):
        loads[k].wait()
        rows = slice(k * half // steps, (k + 1) * half // steps)
        buffer[rows] = buffer[rows] * scale
        stores[k].start()
    for store in stores:
        store.wait()


def graft(own_sums, other_sums, raw):
    steps = 4
    return pl.pallas_call(
        graft_kernel,
        out_shape=jax.ShapeDtypeStruct(raw.shape, jnp.float32),
        in_specs=[vmem(), vmem(), anywhere()],
        out_specs=anywhere(),
        scratch_shapes=[
            pltpu.VMEM(raw.shape, jnp.float32),
            pltpu.SemaphoreType.DMA((steps,)),
            pltpu.SemaphoreType.DMA((steps,)),
        ],
        cost_estimate=pl.CostEstimate(flops=0, bytes_accessed=4 * 2**20, transcendentals=0),
        name="graft",
    )(own_sums, other_sums, raw)


def renew_kernel(
    place_ref, a_ref, nh_ref, nl_ref, fh_ref, fl_ref, out_ref, gh, gl, th, tl
):
    size = a_ref.shape[0]
    half = size // 2
    tiles = size // TILE
    side = place_ref[0]
    used = place_ref[1 + tiles] != 0

    for part, (high_ref, low_ref) in enumerate(((nh_ref, nl_ref), (fh_ref, fl_ref))):
        for r in range(half // TILE):
            for c in range(tiles):
                p = part * (half // TILE) + r
                for source, target, flipped in ((high_ref, gh, th), (low_ref, gl, tl)):
                    block = source[span(r), span(c)]
                    target[span(p), span(c)] = block
                    flipped[span(c), span(p)] = block.T

    def write(i, j, block):
        rows = pl.ds(pl.multiple_of(i * TILE, TILE), TILE)
        cols = pl.ds(pl.multiple_of(j * TILE, TILE), TILE)
        gain = jnp.where(used, block * ((1.0 - decay_rate) / size), 0.0)
        out_ref[rows, cols] = decay_rate * a_ref[rows, cols] + gain

    def products(lh, ll, rh, rl, where):
        for j in range(tiles):
            low_rows = slice(j * TILE, size)
            column = dot3(lh[low_rows, :], ll[low_rows, :], rh[:, span(j)], rl[:, span(j)])
            for i in range(j, tiles):
                block = column[span(i - j)]
                write(where(i), where(j), block)
                if i != j:
                    write(where(j), where(i), block.T)

    @pl.when(side == 0)
    def _():
        products(gh, gl, th, tl, lambda i: place_ref[1 + i])

    @pl.when(side != 0)
    def _():
        products(th, tl, gh, gl, lambda i: i)


def renew(place, factor, near_high, near_low, far_high, far_low):
    size = factor.shape[0]
    return pl.pallas_call(
        renew_kernel,
        out_shape=jax.ShapeDtypeStruct((size, size), jnp.float32),
        in_specs=[smem()] + [vmem()] * 5,
        out_specs=vmem(),
        scratch_shapes=[pltpu.VMEM((size, size), jnp.bfloat16)] * 4,
        compiler_params=pltpu.CompilerParams(vmem_limit_bytes=VMEM_LIMIT),
        cost_estimate=pl.CostEstimate(
            flops=4 * size**3, bytes_accessed=12 * 2**20, transcendentals=0
        ),
        name="renew",
    )(place, factor, near_high, near_low, far_high, far_low)


def per_device(grad, factors, owners):
    row_count = grad.shape[0]
    block_size = factors.shape[-1]
    owner_count = lax.axis_size("block")
    dp_index = lax.axis_index("dp")
    blk_index = lax.axis_index("block")
    side = dp_index % 2
    slot = dp_index // 2
    outer_pair = (dp_index == 0) | (dp_index == 3)
    groups = [
        [x * owner_count + b for x in pair for b in range(owner_count)] for pair in ((0, 3), (1, 2))
    ]

    def exchange(x):
        return lax.all_to_all(
            x, BOTH, split_axis=0, concat_axis=0, tiled=True, axis_index_groups=groups
        )

    def swap(x):
        return lax.ppermute(x, "dp", [(i, i ^ 1) for i in range(4)])

    order = jnp.where(outer_pair, jnp.array([0, 3, 1, 2]), jnp.array([1, 2, 0, 3]))
    used = jnp.sum(owners == blk_index) > slot
    place = jnp.concatenate([side[None], order, used[None]]).astype(jnp.int32)

    other_grad = swap(grad)
    near = exchange(deal(owners, grad, owner_count)).reshape(block_size // 2, block_size)
    own_factor = factors[0, 0]
    x_high, x_low, pack = root(own_factor)
    other_pack = swap(pack)
    dealt = deal(owners, other_grad, owner_count)
    near, dealt = lax.optimization_barrier((near, dealt))
    far = exchange(dealt).reshape(block_size // 2, block_size)

    near_high, near_low, near_sum = split_rows(near)
    v, left_high, left_low, right_high, right_low = near_part(
        place, x_high, x_low, other_pack, near_high, near_low
    )
    raw, far_high, far_low, sums = far_part(
        far, left_high, left_low, v, right_high, right_low, near_sum
    )
    scaled = graft(sums, swap(sums), raw)
    scaled, far_high, far_low = lax.optimization_barrier((scaled, far_high, far_low))
    back = exchange(scaled.reshape(2 * owner_count, row_count, block_size))
    update = collect(owners, back)
    new_own = renew(place, own_factor, near_high, near_low, far_high, far_low)
    return (new_own[None, None], update)


def solution(mesh):
    placed = (P(BOTH, None), P("dp", "block", None, None), P())
    return jax.shard_map(
        per_device,
        mesh=mesh,
        in_specs=placed,
        out_specs=(P("dp", "block", None, None), P(BOTH, None)),
        check_vma=False,
    )
```

```python
import jax
import jax.numpy as jnp
from jax import lax
from jax.experimental import pallas as pl
from jax.experimental.pallas import tpu as pltpu
from jax.sharding import PartitionSpec as P

BOTH = ("dp", "block")
TILE = 256
MIB = 1024 * 1024

decay_rate = 0.9
epsilon = 1e-06


def vmem():
    return pl.BlockSpec(memory_space=pltpu.VMEM)


def anywhere():
    return pl.BlockSpec(memory_space=pl.ANY)


def resident(x):
    return pltpu.with_memory_space_constraint(x, pltpu.VMEM)


def in_hbm(x):
    return pltpu.with_memory_space_constraint(x, pltpu.HBM)


def smem():
    return pl.BlockSpec(memory_space=pltpu.SMEM)


def diag_mask():
    rows = lax.broadcasted_iota(jnp.int32, (TILE, TILE), 0)
    cols = lax.broadcasted_iota(jnp.int32, (TILE, TILE), 1)
    return rows, cols


def span(index):
    return slice(index * TILE, (index + 1) * TILE)


def split(value):
    high = value.astype(jnp.bfloat16)
    low = (value - high.astype(jnp.float32)).astype(jnp.bfloat16)
    return high, low


def dot3(a_high, a_low, b_high, b_low):
    def one(a, b):
        return jnp.dot(a, b, preferred_element_type=jnp.float32)

    return one(a_high, b_high) + (one(a_high, b_low) + one(a_low, b_high))


def put_split(high_ref, low_ref, i, j, block):
    high, low = split(block)
    high_ref[span(i), span(j)] = high
    low_ref[span(i), span(j)] = low


def put_both(high_ref, low_ref, i, j, block):
    put_split(high_ref, low_ref, i, j, block)
    if i != j:
        put_split(high_ref, low_ref, j, i, block.T)


def place_of(owners_ref, count_ref, c):
    owner = owners_ref[c]
    slot = count_ref[owner]
    count_ref[owner] = slot + 1
    return slot * count_ref.shape[0] + owner


def clear(count_ref):
    @pl.loop(0, count_ref.shape[0])
    def _(o):
        count_ref[o] = 0


def column_copies(count, width, source, target, sems):
    each = -(-count // sems.shape[0])
    copies = []
    for k, first in enumerate(range(0, count, each)):
        cols = slice(first * width, min(first + each, count) * width)
        copies.append(pltpu.make_async_copy(source.at[:, cols], target.at[:, cols], sems.at[k]))
    return each, copies


def deal_kernel(owners_ref, grad, out_hbm, count_ref, buffer, sems, whole_sems):
    width = out_hbm.shape[-1]
    count = owners_ref.shape[0]
    each, loads = column_copies(count, width, grad, buffer, whole_sems)
    for load in loads:
        load.start()
    clear(count_ref)
    stores = []
    for c in range(count):
        place = place_of(owners_ref, count_ref, c)
        if c % each == 0:
            loads[c // each].wait()
        cols = slice(c * width, (c + 1) * width)
        stores.append(pltpu.make_async_copy(buffer.at[:, cols], out_hbm.at[place], sems.at[c]))
        stores[-1].start()
    for store in stores:
        store.wait()


def deal_resident_kernel(owners_ref, grad, out_hbm, count_ref, sems):
    width = out_hbm.shape[-1]
    clear(count_ref)
    stores = []
    for c in range(owners_ref.shape[0]):
        place = place_of(owners_ref, count_ref, c)
        cols = slice(c * width, (c + 1) * width)
        stores.append(pltpu.make_async_copy(grad.at[:, cols], out_hbm.at[place], sems.at[c]))
        stores[-1].start()
    for store in stores:
        store.wait()


def collect_kernel(owners_ref, back, out_hbm, count_ref, sems):
    width = back.shape[-1]
    clear(count_ref)
    stores = []
    for c in range(owners_ref.shape[0]):
        place = place_of(owners_ref, count_ref, c)
        cols = slice(c * width, (c + 1) * width)
        stores.append(pltpu.make_async_copy(back.at[place], out_hbm.at[:, cols], sems.at[c]))
        stores[-1].start()
    for store in stores:
        store.wait()


def deal(owners, grad, owner_count, landed):
    rows = grad.shape[0]
    count = owners.shape[0]
    width = grad.shape[1] // count
    counts, sems = pltpu.SMEM((owner_count,), jnp.int32), pltpu.SemaphoreType.DMA((count,))
    buffers = [pltpu.VMEM(grad.shape, jnp.float32), sems, pltpu.SemaphoreType.DMA((4,))]
    return pl.pallas_call(
        deal_resident_kernel if landed else deal_kernel,
        out_shape=pltpu.HBM((2 * owner_count, rows, width), jnp.float32),
        in_specs=[smem(), vmem() if landed else anywhere()],
        out_specs=anywhere(),
        scratch_shapes=[counts, sems] if landed else [counts] + buffers,
        compiler_params=pltpu.CompilerParams(vmem_limit_bytes=16 * MIB),
        cost_estimate=pl.CostEstimate(flops=5 * 10**10, bytes_accessed=2**22, transcendentals=0),
        name="deal",
    )(owners, resident(grad) if landed else in_hbm(grad))


def collect(owners, back):
    places, rows, width = back.shape
    return pl.pallas_call(
        collect_kernel,
        out_shape=jax.ShapeDtypeStruct((rows, owners.shape[0] * width), jnp.float32),
        in_specs=[smem(), vmem()],
        out_specs=anywhere(),
        scratch_shapes=[
            pltpu.SMEM((places // 2,), jnp.int32),
            pltpu.SemaphoreType.DMA((owners.shape[0],)),
        ],
        compiler_params=pltpu.CompilerParams(vmem_limit_bytes=16 * MIB),
        cost_estimate=pl.CostEstimate(flops=0, bytes_accessed=2**22, transcendentals=0),
        name="collect",
    )(owners, resident(back))


def lower_blocks(tiles):
    return [(i, j) for j in range(tiles) for i in range(j + 1, tiles)]


def root_kernel(
    a_hbm, xh_hbm, xl_hbm, pack_hbm,
    a, sh, sl, s2, s2h, s2l, s3h, s3l, qh, ql, xh, xl, pack, in_sems, out_sems,
):
    size = a.shape[0]
    tiles = size // TILE
    rows, cols = diag_mask()
    on_diag = rows == cols
    loads = [
        pltpu.make_async_copy(a_hbm.at[span(b)], a.at[span(b)], in_sems.at[b]) for b in range(tiles)
    ]
    for load in loads:
        load.start()
    diagonal = jnp.zeros((8, TILE), jnp.float32)
    for b in range(tiles):
        loads[b].wait()
        block = jnp.where(on_diag, a[span(b), span(b)], 0.0)
        diagonal += jnp.sum(block.reshape(TILE // 8, 8, TILE), axis=0)
    shrink = 0.25 / (2.0 * jnp.sum(diagonal) / size)

    def step_block(i, j):
        block = a[span(i), span(j)] * -shrink
        if i == j:
            block = jnp.where(on_diag, 1.25 + block, block)
        return block

    for i in range(tiles):
        for j in range(tiles):
            put_split(sh, sl, i, j, step_block(i, j))

    def product(ah, al, bh, bl, j):
        low_rows = slice(j * TILE, size)
        return dot3(ah[low_rows, :], al[low_rows, :], bh[:, span(j)], bl[:, span(j)])

    for j in range(tiles):
        column = product(sh, sl, sh, sl, j)
        s2[j * TILE :, span(j)] = column
        for i in range(j, tiles):
            put_both(s2h, s2l, i, j, column[span(i - j)])
    for j in range(tiles):
        column = product(sh, sl, s2h, s2l, j)
        for i in range(j, tiles):
            block = column[span(i - j)]
            put_both(s3h, s3l, i, j, block)
            put_both(qh, ql, i, j, block - 1.25 * s2[span(i), span(j)])

    stores = []

    def store(source, target, where):
        k = len(stores)
        stores.append(pltpu.make_async_copy(source.at[where], target.at[where], out_sems.at[k]))
        stores[-1].start()

    offset = len(lower_blocks(tiles))
    last = (offset + tiles // 2) * TILE
    for j in range(tiles):
        column = product(s3h, s3l, qh, ql, j)
        for i in range(j, tiles):
            block = column[span(i - j)] + 1.25 * step_block(i, j)
            put_both(xh, xl, i, j, block)
            if i != j:
                pack[span(lower_blocks(tiles).index((i, j)))] = block
            else:
                s2[span(i), span(i)] = block
        if j + 1 < tiles:
            first = lower_blocks(tiles).index((j + 1, j))
            store(pack, pack_hbm, slice(first * TILE, (first + tiles - 1 - j) * TILE))
        if j % 2:
            first, second = s2[span(j - 1), span(j - 1)], s2[span(j), span(j)]
            pack[span(offset + j // 2)] = jnp.where(rows >= cols, first, second)
            line = jnp.sum(jnp.where(on_diag, second, 0.0), axis=0, keepdims=True)
            start = last + j // 2 * 8
            pack[start : start + 8] = jnp.broadcast_to(line, (8, TILE))
            store(pack, pack_hbm, span(offset + j // 2))
            store(pack, pack_hbm, slice(start, start + 8))
        store(xh, xh_hbm, span(j))
        store(xl, xl_hbm, span(j))
    for copy in stores:
        copy.wait()


def packed_rows(size):
    tiles = size // TILE
    return (len(lower_blocks(tiles)) + tiles // 2) * TILE + 8 * (tiles // 2)


def root(factor):
    size = factor.shape[0]
    tiles = size // TILE
    half = pltpu.HBM((size, size), jnp.bfloat16)
    square = pltpu.VMEM((size, size), jnp.float32)
    square_half = pltpu.VMEM((size, size), jnp.bfloat16)
    packed = (packed_rows(size), TILE)
    return pl.pallas_call(
        root_kernel,
        out_shape=[half, half, pltpu.HBM(packed, jnp.float32)],
        in_specs=[anywhere()],
        out_specs=[anywhere()] * 3,
        scratch_shapes=[square, square_half, square_half, square]
        + [square_half] * 8
        + [
            pltpu.VMEM(packed, jnp.float32),
            pltpu.SemaphoreType.DMA((tiles,)),
            pltpu.SemaphoreType.DMA((4 * tiles - 1,)),
        ],
        compiler_params=pltpu.CompilerParams(vmem_limit_bytes=44 * MIB),
        cost_estimate=pl.CostEstimate(flops=0, bytes_accessed=0, transcendentals=0),
        name="root",
    )(in_hbm(factor))


def unpack_block(pack_ref, tiles, i, j, rows, cols):
    if i != j:
        return pack_ref[span(lower_blocks(tiles).index((i, j)))]
    offset = len(lower_blocks(tiles))
    last = (offset + tiles // 2) * TILE
    both = pack_ref[span(offset + i // 2)]
    if i % 2 == 0:
        return jnp.where(rows >= cols, both, both.T)
    diagonal = pack_ref[last + (i // 2) * 8 : last + (i // 2) * 8 + 1]
    return jnp.where(rows == cols, diagonal, jnp.where(rows < cols, both, both.T))


def split_kernel(x_ref, high_ref, low_ref, sum_ref):
    half, size = x_ref.shape
    total = jnp.zeros((8, TILE), jnp.float32)
    for r in range(half // TILE):
        for c in range(size // TILE):
            block = x_ref[span(r), span(c)]
            put_split(high_ref, low_ref, r, c, block)
            total += jnp.sum((block * block).reshape(TILE // 8, 8, TILE), axis=0)
    sum_ref[...] = jnp.full(sum_ref.shape, jnp.sum(total), jnp.float32)


def split_rows(x):
    half = pltpu.HBM(x.shape, jnp.bfloat16)
    return pl.pallas_call(
        split_kernel,
        out_shape=[half, half, jax.ShapeDtypeStruct((8, 128), jnp.float32)],
        in_specs=[vmem()],
        out_specs=[vmem()] * 3,
        compiler_params=pltpu.CompilerParams(vmem_limit_bytes=56 * MIB),
        cost_estimate=pl.CostEstimate(flops=0, bytes_accessed=4 * 2**20, transcendentals=0),
        name="split_rows",
    )(in_hbm(x))


def raw_kernel(
    place_ref, near_sum_ref, xh_hbm, xl_hbm, pack, nh_hbm, nl_hbm, far, raw, sums_ref,
    xh, xl, nh, nl, ph, pw, fh, fl, lh, ll, uh, ul, sems,
):
    half, size = far.shape
    tiles = size // TILE
    split_at = half // TILE
    side = place_ref[0]
    rows, cols = diag_mask()
    sources, targets = (nh_hbm, nl_hbm, xh_hbm, xl_hbm), (nh, nl, xh, xl)
    loads = [
        pltpu.make_async_copy(source, target, sems.at[k])
        for k, (source, target) in enumerate(zip(sources, targets))
    ]
    for load in loads:
        load.start()

    def own_arrived():
        for load in loads[2:]:
            load.wait()

    for i in range(tiles):
        for j in range(i + 1):
            put_both(ph, pw, i, j, unpack_block(pack, tiles, i, j, rows, cols))

    def place_left(high_ref, low_ref):
        for r in range(split_at):
            source_rows = pl.ds(pl.multiple_of(place_ref[1 + r] * TILE, TILE), TILE)
            for c in range(tiles):
                source_cols = pl.ds(pl.multiple_of(place_ref[1 + c] * TILE, TILE), TILE)
                lh[c // split_at, span(r), span(c % split_at)] = high_ref[source_rows, source_cols]
                ll[c // split_at, span(r), span(c % split_at)] = low_ref[source_rows, source_cols]

    @pl.when(side == 0)
    def _():
        own_arrived()
        place_left(xh, xl)

    @pl.when(side != 0)
    def _():
        place_left(ph, pw)

    for load in loads[:2]:
        load.wait()

    total = jnp.zeros((8, TILE), jnp.float32)
    for j in range(tiles):
        block = far[:, span(j)]
        fh[:, span(j)], fl[:, span(j)] = split(block)
        total += jnp.sum((block * block).reshape(half // 8, 8, TILE), axis=0)
        column = dot3(lh[0], ll[0], nh[:, span(j)], nl[:, span(j)])
        column += dot3(lh[1], ll[1], fh[:, span(j)], fl[:, span(j)])
        uh[:, span(j)], ul[:, span(j)] = split(column)
    grad_sum = jnp.sum(total) + near_sum_ref[0, 0]

    def times_right(high_ref, low_ref):
        total = jnp.zeros((8, TILE), jnp.float32)
        for j in range(tiles):
            column = dot3(uh[...], ul[...], high_ref[:, span(j)], low_ref[:, span(j)])
            raw[:, span(j)] = column
            total += jnp.sum((column * column).reshape(half // 8, 8, TILE), axis=0)
        lane = lax.broadcasted_iota(jnp.int32, (8, 128), 1)
        sums_ref[...] = jnp.where(lane == 0, jnp.sum(total), grad_sum)

    @pl.when(side == 0)
    def _():
        times_right(ph, pw)

    @pl.when(side != 0)
    def _():
        own_arrived()
        times_right(xh, xl)


def raw_rows(place, near_sum, x_high, x_low, pack, near_high, near_low, far):
    half, size = far.shape
    wide = pltpu.VMEM((half, size), jnp.bfloat16)
    big = pltpu.VMEM((size, size), jnp.bfloat16)
    two = pltpu.VMEM((2, half, half), jnp.bfloat16)
    return pl.pallas_call(
        raw_kernel,
        out_shape=[
            pltpu.VMEM((half, size), jnp.float32),
            jax.ShapeDtypeStruct((8, 128), jnp.float32),
        ],
        in_specs=[smem(), vmem(), anywhere(), anywhere(), vmem(), anywhere(), anywhere(), vmem()],
        out_specs=[vmem(), vmem()],
        scratch_shapes=[
            big, big, wide, wide, big, big, wide, wide, two, two, wide, wide,
            pltpu.SemaphoreType.DMA((4,)),
        ],
        compiler_params=pltpu.CompilerParams(vmem_limit_bytes=40 * MIB),
        cost_estimate=pl.CostEstimate(
            flops=6 * size**3, bytes_accessed=12 * 2**20, transcendentals=0
        ),
        name="raw_rows",
    )(
        place, near_sum, in_hbm(x_high), in_hbm(x_low), resident(pack),
        in_hbm(near_high), in_hbm(near_low), resident(far),
    )


def graft_kernel(own_ref, other_ref, raw, out_hbm, buffer, sems):
    half, size = buffer.shape
    steps = sems.shape[0]
    count = size * size
    own = own_ref[...]
    raw_sum = own[:1, :1] + other_ref[:1, :1]
    grad_sum = own[:1, 1:2]
    scale = jnp.sqrt(grad_sum / count + epsilon) / jnp.sqrt(raw_sum / count + epsilon)
    stores = []
    for k in range(steps):
        rows = slice(k * half // steps, (k + 1) * half // steps)
        buffer[rows] = raw[rows] * scale
        stores.append(pltpu.make_async_copy(buffer.at[rows], out_hbm.at[rows], sems.at[k]))
        stores[-1].start()
    for store in stores:
        store.wait()


def graft(own_sums, other_sums, raw):
    steps = 4
    return pl.pallas_call(
        graft_kernel,
        out_shape=pltpu.HBM(raw.shape, jnp.float32),
        in_specs=[vmem(), vmem(), vmem()],
        out_specs=anywhere(),
        scratch_shapes=[
            pltpu.VMEM(raw.shape, jnp.float32),
            pltpu.SemaphoreType.DMA((steps,)),
        ],
        compiler_params=pltpu.CompilerParams(vmem_limit_bytes=6 * MIB),
        cost_estimate=pl.CostEstimate(flops=0, bytes_accessed=4 * 2**20, transcendentals=0),
        name="graft",
    )(own_sums, other_sums, resident(raw))


def renew_kernel(
    place_ref, a_ref, nh_ref, nl_ref, far_ref, out_ref, gh, gl, th, tl
):
    size = a_ref.shape[0]
    half = size // 2
    tiles = size // TILE
    side = place_ref[0]
    used = place_ref[1 + tiles] != 0

    for p in range(tiles):
        for c in range(tiles):
            if p < half // TILE:
                high, low = nh_ref[span(p), span(c)], nl_ref[span(p), span(c)]
            else:
                high, low = split(far_ref[span(p - half // TILE), span(c)])
            for block, target, flipped in ((high, gh, th), (low, gl, tl)):
                target[span(p), span(c)] = block
                flipped[span(c), span(p)] = block.T

    def write(i, j, block):
        rows = pl.ds(pl.multiple_of(i * TILE, TILE), TILE)
        cols = pl.ds(pl.multiple_of(j * TILE, TILE), TILE)
        gain = jnp.where(used, block * ((1.0 - decay_rate) / size), 0.0)
        out_ref[rows, cols] = decay_rate * a_ref[rows, cols] + gain

    def products(lh, ll, rh, rl, where):
        for j in range(tiles):
            low_rows = slice(j * TILE, size)
            column = dot3(lh[low_rows, :], ll[low_rows, :], rh[:, span(j)], rl[:, span(j)])
            for i in range(j, tiles):
                block = column[span(i - j)]
                write(where(i), where(j), block)
                if i != j:
                    write(where(j), where(i), block.T)

    @pl.when(side == 0)
    def _():
        products(gh, gl, th, tl, lambda i: place_ref[1 + i])

    @pl.when(side != 0)
    def _():
        products(th, tl, gh, gl, lambda i: i)


def renew(place, factor, near_high, near_low, far):
    size = factor.shape[0]
    return pl.pallas_call(
        renew_kernel,
        out_shape=jax.ShapeDtypeStruct((size, size), jnp.float32),
        in_specs=[smem()] + [vmem()] * 4,
        out_specs=vmem(),
        scratch_shapes=[pltpu.VMEM((size, size), jnp.bfloat16)] * 4,
        compiler_params=pltpu.CompilerParams(vmem_limit_bytes=56 * MIB),
        cost_estimate=pl.CostEstimate(
            flops=4 * size**3, bytes_accessed=12 * 2**20, transcendentals=0
        ),
        name="renew",
    )(place, factor, near_high, near_low, far)


def per_device(grad, factors, owners):
    row_count = grad.shape[0]
    block_size = factors.shape[-1]
    owner_count = lax.axis_size("block")
    dp_index = lax.axis_index("dp")
    blk_index = lax.axis_index("block")
    side = dp_index % 2
    slot = dp_index // 2
    outer_pair = (dp_index == 0) | (dp_index == 3)
    groups = [
        [x * owner_count + b for x in pair for b in range(owner_count)] for pair in ((0, 3), (1, 2))
    ]

    def exchange(x):
        return lax.all_to_all(
            x, BOTH, split_axis=0, concat_axis=0, tiled=True, axis_index_groups=groups
        )

    def swap(x):
        return lax.ppermute(x, "dp", [(i, i ^ 1) for i in range(4)])

    order = jnp.where(outer_pair, jnp.array([0, 3, 1, 2]), jnp.array([1, 2, 0, 3]))
    used = jnp.sum(owners == blk_index) > slot
    place = jnp.concatenate([side[None], order, used[None]]).astype(jnp.int32)

    near = exchange(deal(owners, grad, owner_count, False)).reshape(block_size // 2, block_size)
    other_grad = swap(grad)
    own_factor = factors[0, 0]
    x_high, x_low, pack = root(own_factor)
    other_pack = swap(pack)
    dealt = deal(owners, other_grad, owner_count, True)
    near, dealt = lax.optimization_barrier((near, dealt))
    far = exchange(dealt).reshape(block_size // 2, block_size)

    near_high, near_low, near_sum = split_rows(near)
    raw, sums = raw_rows(place, near_sum, x_high, x_low, other_pack, near_high, near_low, far)
    scaled = graft(sums, swap(sums), raw)
    scaled, far = lax.optimization_barrier((scaled, far))
    back = exchange(scaled.reshape(2 * owner_count, row_count, block_size))
    update = collect(owners, back)
    new_own = renew(place, own_factor, near_high, near_low, far)
    return (new_own[None, None], update)


def solution(mesh):
    placed = (P(BOTH, None), P("dp", "block", None, None), P())
    return jax.shard_map(
        per_device,
        mesh=mesh,
        in_specs=placed,
        out_specs=(P("dp", "block", None, None), P(BOTH, None)),
        check_vma=False,
    )
```

```python
import jax
import jax.numpy as jnp
from jax import lax
from jax.experimental import pallas as pl
from jax.experimental.pallas import tpu as pltpu
from jax.sharding import PartitionSpec as P

BOTH = ("dp", "block")
TILE = 256
MIB = 1024 * 1024

decay_rate = 0.9
epsilon = 1e-06


def vmem():
    return pl.BlockSpec(memory_space=pltpu.VMEM)


def anywhere():
    return pl.BlockSpec(memory_space=pl.ANY)


def resident(x):
    return pltpu.with_memory_space_constraint(x, pltpu.VMEM)


def in_hbm(x):
    return pltpu.with_memory_space_constraint(x, pltpu.HBM)


def smem():
    return pl.BlockSpec(memory_space=pltpu.SMEM)


def diag_mask():
    rows = lax.broadcasted_iota(jnp.int32, (TILE, TILE), 0)
    cols = lax.broadcasted_iota(jnp.int32, (TILE, TILE), 1)
    return rows, cols


def span(index):
    return slice(index * TILE, (index + 1) * TILE)


def split(value):
    high = value.astype(jnp.bfloat16)
    low = (value - high.astype(jnp.float32)).astype(jnp.bfloat16)
    return high, low


def dot3(a_high, a_low, b_high, b_low):
    def one(a, b):
        return jnp.dot(a, b, preferred_element_type=jnp.float32)

    return one(a_high, b_high) + (one(a_high, b_low) + one(a_low, b_high))


def put_split(high_ref, low_ref, i, j, block):
    high, low = split(block)
    high_ref[span(i), span(j)] = high
    low_ref[span(i), span(j)] = low


def put_both(high_ref, low_ref, i, j, block):
    put_split(high_ref, low_ref, i, j, block)
    if i != j:
        put_split(high_ref, low_ref, j, i, block.T)


def place_of(owners_ref, count_ref, c):
    owner = owners_ref[c]
    slot = count_ref[owner]
    count_ref[owner] = slot + 1
    return slot * count_ref.shape[0] + owner


def clear(count_ref):
    @pl.loop(0, count_ref.shape[0])
    def _(o):
        count_ref[o] = 0


def column_copies(count, width, source, target, sems):
    each = -(-count // sems.shape[0])
    copies = []
    for k, first in enumerate(range(0, count, each)):
        cols = slice(first * width, min(first + each, count) * width)
        copies.append(pltpu.make_async_copy(source.at[:, cols], target.at[:, cols], sems.at[k]))
    return each, copies


def deal_kernel(owners_ref, grad, out_hbm, count_ref, buffer, sems, whole_sems):
    width = out_hbm.shape[-1]
    count = owners_ref.shape[0]
    each, loads = column_copies(count, width, grad, buffer, whole_sems)
    for load in loads:
        load.start()
    clear(count_ref)
    stores = []
    for c in range(count):
        place = place_of(owners_ref, count_ref, c)
        if c % each == 0:
            loads[c // each].wait()
        cols = slice(c * width, (c + 1) * width)
        stores.append(pltpu.make_async_copy(buffer.at[:, cols], out_hbm.at[place], sems.at[c]))
        stores[-1].start()
    for store in stores:
        store.wait()


def deal_resident_kernel(owners_ref, grad, out_hbm, count_ref, sems):
    width = out_hbm.shape[-1]
    clear(count_ref)
    stores = []
    for c in range(owners_ref.shape[0]):
        place = place_of(owners_ref, count_ref, c)
        cols = slice(c * width, (c + 1) * width)
        stores.append(pltpu.make_async_copy(grad.at[:, cols], out_hbm.at[place], sems.at[c]))
        stores[-1].start()
    for store in stores:
        store.wait()


def collect_kernel(owners_ref, back, out_hbm, count_ref, sems):
    width = back.shape[-1]
    clear(count_ref)
    stores = []
    for c in range(owners_ref.shape[0]):
        place = place_of(owners_ref, count_ref, c)
        cols = slice(c * width, (c + 1) * width)
        stores.append(pltpu.make_async_copy(back.at[place], out_hbm.at[:, cols], sems.at[c]))
        stores[-1].start()
    for store in stores:
        store.wait()


def deal(owners, grad, owner_count, landed):
    rows = grad.shape[0]
    count = owners.shape[0]
    width = grad.shape[1] // count
    counts, sems = pltpu.SMEM((owner_count,), jnp.int32), pltpu.SemaphoreType.DMA((count,))
    buffers = [pltpu.VMEM(grad.shape, jnp.float32), sems, pltpu.SemaphoreType.DMA((4,))]
    return pl.pallas_call(
        deal_resident_kernel if landed else deal_kernel,
        out_shape=pltpu.HBM((2 * owner_count, rows, width), jnp.float32),
        in_specs=[smem(), vmem() if landed else anywhere()],
        out_specs=anywhere(),
        scratch_shapes=[counts, sems] if landed else [counts] + buffers,
        compiler_params=pltpu.CompilerParams(vmem_limit_bytes=16 * MIB),
        cost_estimate=pl.CostEstimate(flops=5 * 10**10, bytes_accessed=2**22, transcendentals=0),
        name="deal",
    )(owners, resident(grad) if landed else in_hbm(grad))


def collect(owners, back):
    places, rows, width = back.shape
    return pl.pallas_call(
        collect_kernel,
        out_shape=jax.ShapeDtypeStruct((rows, owners.shape[0] * width), jnp.float32),
        in_specs=[smem(), vmem()],
        out_specs=anywhere(),
        scratch_shapes=[
            pltpu.SMEM((places // 2,), jnp.int32),
            pltpu.SemaphoreType.DMA((owners.shape[0],)),
        ],
        compiler_params=pltpu.CompilerParams(vmem_limit_bytes=16 * MIB),
        cost_estimate=pl.CostEstimate(flops=0, bytes_accessed=2**22, transcendentals=0),
        name="collect",
    )(owners, resident(back))


def lower_blocks(tiles):
    return [(i, j) for j in range(tiles) for i in range(j + 1, tiles)]


def root_kernel(
    a_hbm, xh_hbm, xl_hbm, pack_hbm,
    a, sh, sl, s2, s2h, s2l, s3h, s3l, qh, ql, xh, xl, pack, in_sems, out_sems,
):
    size = a.shape[0]
    tiles = size // TILE
    rows, cols = diag_mask()
    on_diag = rows == cols
    loads = [
        pltpu.make_async_copy(a_hbm.at[span(b)], a.at[span(b)], in_sems.at[b]) for b in range(tiles)
    ]
    for load in loads:
        load.start()
    diagonal = jnp.zeros((8, TILE), jnp.float32)
    for b in range(tiles):
        loads[b].wait()
        block = jnp.where(on_diag, a[span(b), span(b)], 0.0)
        diagonal += jnp.sum(block.reshape(TILE // 8, 8, TILE), axis=0)
    shrink = 0.25 / (2.0 * jnp.sum(diagonal) / size)

    def step_block(i, j):
        block = a[span(i), span(j)] * -shrink
        if i == j:
            block = jnp.where(on_diag, 1.25 + block, block)
        return block

    for i in range(tiles):
        for j in range(tiles):
            put_split(sh, sl, i, j, step_block(i, j))

    def product(ah, al, bh, bl, j):
        low_rows = slice(j * TILE, size)
        return dot3(ah[low_rows, :], al[low_rows, :], bh[:, span(j)], bl[:, span(j)])

    for j in range(tiles):
        column = product(sh, sl, sh, sl, j)
        s2[j * TILE :, span(j)] = column
        for i in range(j, tiles):
            put_both(s2h, s2l, i, j, column[span(i - j)])
    for j in range(tiles):
        column = product(sh, sl, s2h, s2l, j)
        for i in range(j, tiles):
            block = column[span(i - j)]
            put_both(s3h, s3l, i, j, block)
            put_both(qh, ql, i, j, block - 1.25 * s2[span(i), span(j)])

    stores = []

    def store(source, target, where):
        k = len(stores)
        stores.append(pltpu.make_async_copy(source.at[where], target.at[where], out_sems.at[k]))
        stores[-1].start()

    offset = len(lower_blocks(tiles))
    last = (offset + tiles // 2) * TILE
    for j in range(tiles):
        column = product(s3h, s3l, qh, ql, j)
        for i in range(j, tiles):
            block = column[span(i - j)] + 1.25 * step_block(i, j)
            put_both(xh, xl, i, j, block)
            if i != j:
                pack[span(lower_blocks(tiles).index((i, j)))] = block
            else:
                s2[span(i), span(i)] = block
        if j + 1 < tiles:
            first = lower_blocks(tiles).index((j + 1, j))
            store(pack, pack_hbm, slice(first * TILE, (first + tiles - 1 - j) * TILE))
        if j % 2:
            first, second = s2[span(j - 1), span(j - 1)], s2[span(j), span(j)]
            pack[span(offset + j // 2)] = jnp.where(rows >= cols, first, second)
            line = jnp.sum(jnp.where(on_diag, second, 0.0), axis=0, keepdims=True)
            start = last + j // 2 * 8
            pack[start : start + 8] = jnp.broadcast_to(line, (8, TILE))
            store(pack, pack_hbm, span(offset + j // 2))
            store(pack, pack_hbm, slice(start, start + 8))
        store(xh, xh_hbm, span(j))
        store(xl, xl_hbm, span(j))
    for copy in stores:
        copy.wait()


def packed_rows(size):
    tiles = size // TILE
    return (len(lower_blocks(tiles)) + tiles // 2) * TILE + 8 * (tiles // 2)


def root(factor):
    size = factor.shape[0]
    tiles = size // TILE
    half = pltpu.HBM((size, size), jnp.bfloat16)
    square = pltpu.VMEM((size, size), jnp.float32)
    square_half = pltpu.VMEM((size, size), jnp.bfloat16)
    packed = (packed_rows(size), TILE)
    return pl.pallas_call(
        root_kernel,
        out_shape=[half, half, pltpu.HBM(packed, jnp.float32)],
        in_specs=[anywhere()],
        out_specs=[anywhere()] * 3,
        scratch_shapes=[square, square_half, square_half, square]
        + [square_half] * 8
        + [
            pltpu.VMEM(packed, jnp.float32),
            pltpu.SemaphoreType.DMA((tiles,)),
            pltpu.SemaphoreType.DMA((4 * tiles - 1,)),
        ],
        compiler_params=pltpu.CompilerParams(vmem_limit_bytes=44 * MIB),
        cost_estimate=pl.CostEstimate(flops=0, bytes_accessed=0, transcendentals=0),
        name="root",
    )(in_hbm(factor))


def unpack_block(pack_ref, tiles, i, j, rows, cols):
    if i != j:
        return pack_ref[span(lower_blocks(tiles).index((i, j)))]
    offset = len(lower_blocks(tiles))
    last = (offset + tiles // 2) * TILE
    both = pack_ref[span(offset + i // 2)]
    if i % 2 == 0:
        return jnp.where(rows >= cols, both, both.T)
    diagonal = pack_ref[last + (i // 2) * 8 : last + (i // 2) * 8 + 1]
    return jnp.where(rows == cols, diagonal, jnp.where(rows < cols, both, both.T))


def unpack(pack_ref, tiles, high_ref, low_ref):
    rows, cols = diag_mask()
    for i in range(tiles):
        for j in range(i + 1):
            put_both(high_ref, low_ref, i, j, unpack_block(pack_ref, tiles, i, j, rows, cols))


def squares(block):
    return jnp.sum((block * block).reshape(block.shape[0] // 8, 8, TILE), axis=0)


def place_left(place_ref, parts, tiles, high_ref, low_ref, lh, ll):
    for r in range(tiles // 2):
        source_rows = pl.ds(pl.multiple_of(place_ref[1 + r] * TILE, TILE), TILE)
        for c in range(parts[0], parts[1]):
            source_cols = pl.ds(pl.multiple_of(place_ref[1 + c] * TILE, TILE), TILE)
            lh[span(r), span(c - parts[0])] = high_ref[source_rows, source_cols]
            ll[span(r), span(c - parts[0])] = low_ref[source_rows, source_cols]


def early_kernel(place_ref, near, xh, xl, out, nh, nl, sum_ref, lh, ll):
    half, size = near.shape
    tiles = size // TILE
    side = place_ref[0]
    total = jnp.zeros((8, TILE), jnp.float32)
    for j in range(tiles):
        block = near[:, span(j)]
        nh[:, span(j)], nl[:, span(j)] = split(block)
        total += squares(block)
    sum_ref[...] = jnp.full(sum_ref.shape, jnp.sum(total), jnp.float32)

    @pl.when(side == 0)
    def _():
        place_left(place_ref, (0, tiles // 2), tiles, xh, xl, lh, ll)
        for j in range(tiles):
            out[:, span(j)] = dot3(lh[...], ll[...], nh[:, span(j)], nl[:, span(j)])

    @pl.when(side != 0)
    def _():
        for j in range(tiles):
            out[:, span(j)] = dot3(nh[...], nl[...], xh[:, span(j)], xl[:, span(j)])


def early_part(place, near, x_high, x_low):
    half, size = near.shape
    square = pltpu.VMEM((half, half), jnp.bfloat16)
    rows = pltpu.HBM((half, size), jnp.bfloat16)
    return pl.pallas_call(
        early_kernel,
        out_shape=[
            pltpu.HBM((half, size), jnp.float32), rows, rows,
            pltpu.HBM((8, 128), jnp.float32),
        ],
        in_specs=[smem()] + [vmem()] * 3,
        out_specs=[vmem()] * 4,
        scratch_shapes=[square, square],
        compiler_params=pltpu.CompilerParams(vmem_limit_bytes=56 * MIB),
        cost_estimate=pl.CostEstimate(flops=0, bytes_accessed=0, transcendentals=0),
        name="early_part",
    )(place, in_hbm(near), in_hbm(x_high), in_hbm(x_low))


def middle_kernel(
    place_ref, near_sum_hbm, far, early_hbm, pack_hbm, yh, yl, sum_ref,
    near_sum, early, pack, xh, xl, fh, fl, lh, ll, sems,
):
    half, size = far.shape
    tiles = size // TILE
    side = place_ref[0]
    pack_load = pltpu.make_async_copy(pack_hbm, pack, sems.at[0])
    early_load = pltpu.make_async_copy(early_hbm, early, sems.at[1])
    sum_load = pltpu.make_async_copy(near_sum_hbm, near_sum, sems.at[2])
    for load in (pack_load, early_load, sum_load):
        load.start()
    total = jnp.zeros((8, TILE), jnp.float32)
    for j in range(tiles):
        block = far[:, span(j)]
        fh[:, span(j)], fl[:, span(j)] = split(block)
        total += squares(block)
    pack_load.wait()
    unpack(pack, tiles, xh, xl)
    sum_load.wait()
    sum_ref[...] = near_sum[...] + jnp.sum(total)

    @pl.when(side == 0)
    def _():
        place_left(place_ref, (tiles // 2, tiles), tiles, xh, xl, lh, ll)
        early_load.wait()
        for j in range(tiles):
            column = early[:, span(j)] + dot3(lh[...], ll[...], fh[:, span(j)], fl[:, span(j)])
            yh[:half, span(j)], yl[:half, span(j)] = split(column)

    @pl.when(side != 0)
    def _():
        for j in range(tiles):
            column = dot3(fh[...], fl[...], xh[:, span(j)], xl[:, span(j)])
            yh[half:, span(j)], yl[half:, span(j)] = split(column)
        early_load.wait()
        for j in range(tiles):
            yh[:half, span(j)], yl[:half, span(j)] = split(early[:, span(j)])


def middle_part(place, near_sum, far, early, pack):
    half, size = far.shape
    wide = pltpu.VMEM((half, size), jnp.bfloat16)
    square = pltpu.VMEM((half, half), jnp.bfloat16)
    big = pltpu.VMEM((size, size), jnp.bfloat16)
    return pl.pallas_call(
        middle_kernel,
        out_shape=[big, big, jax.ShapeDtypeStruct((8, 128), jnp.float32)],
        in_specs=[smem(), anywhere(), vmem(), anywhere(), anywhere()],
        out_specs=[vmem()] * 3,
        scratch_shapes=[
            pltpu.VMEM(near_sum.shape, jnp.float32),
            pltpu.VMEM((half, size), jnp.float32),
            pltpu.VMEM(pack.shape, jnp.float32),
            big, big, wide, wide, square, square,
            pltpu.SemaphoreType.DMA((3,)),
        ],
        compiler_params=pltpu.CompilerParams(vmem_limit_bytes=24 * MIB),
        cost_estimate=pl.CostEstimate(flops=0, bytes_accessed=0, transcendentals=0),
        name="middle_part",
    )(place, in_hbm(near_sum), resident(far), in_hbm(early), in_hbm(pack))


def last_kernel(place_ref, grad_sum_ref, yh, yl, pack, raw, sums_ref, ph, pw, lh, ll):
    half, size = raw.shape
    tiles = size // TILE
    side = place_ref[0]
    unpack(pack, tiles, ph, pw)

    def multiply(ah, al, bh, bl):
        total = jnp.zeros((8, TILE), jnp.float32)
        for j in range(tiles):
            column = dot3(ah, al, bh[:, span(j)], bl[:, span(j)])
            raw[:, span(j)] = column
            total += squares(column)
        lane = lax.broadcasted_iota(jnp.int32, (8, 128), 1)
        sums_ref[...] = jnp.where(lane == 0, jnp.sum(total), grad_sum_ref[...])

    @pl.when(side == 0)
    def _():
        multiply(yh[:half], yl[:half], ph, pw)

    @pl.when(side != 0)
    def _():
        place_left(place_ref, (0, tiles), tiles, ph, pw, lh, ll)
        multiply(lh[...], ll[...], yh, yl)


def last_part(place, grad_sum, y_high, y_low, pack):
    size = y_high.shape[0]
    half = size // 2
    wide = pltpu.VMEM((half, size), jnp.bfloat16)
    big = pltpu.VMEM((size, size), jnp.bfloat16)
    return pl.pallas_call(
        last_kernel,
        out_shape=[
            pltpu.VMEM((half, size), jnp.float32),
            jax.ShapeDtypeStruct((8, 128), jnp.float32),
        ],
        in_specs=[smem()] + [vmem()] * 4,
        out_specs=[vmem(), vmem()],
        scratch_shapes=[big, big, wide, wide],
        compiler_params=pltpu.CompilerParams(vmem_limit_bytes=32 * MIB),
        cost_estimate=pl.CostEstimate(
            flops=3 * size**3, bytes_accessed=12 * 2**20, transcendentals=0
        ),
        name="last_part",
    )(place, grad_sum, resident(y_high), resident(y_low), resident(pack))


def graft_kernel(own_ref, other_ref, raw, out_hbm, buffer, sems):
    half, size = buffer.shape
    steps = sems.shape[0]
    count = size * size
    own = own_ref[...]
    raw_sum = own[:1, :1] + other_ref[:1, :1]
    grad_sum = own[:1, 1:2]
    scale = jnp.sqrt(grad_sum / count + epsilon) / jnp.sqrt(raw_sum / count + epsilon)
    stores = []
    for k in range(steps):
        rows = slice(k * half // steps, (k + 1) * half // steps)
        buffer[rows] = raw[rows] * scale
        stores.append(pltpu.make_async_copy(buffer.at[rows], out_hbm.at[rows], sems.at[k]))
        stores[-1].start()
    for store in stores:
        store.wait()


def graft(own_sums, other_sums, raw):
    steps = 4
    return pl.pallas_call(
        graft_kernel,
        out_shape=pltpu.HBM(raw.shape, jnp.float32),
        in_specs=[vmem(), vmem(), vmem()],
        out_specs=anywhere(),
        scratch_shapes=[
            pltpu.VMEM(raw.shape, jnp.float32),
            pltpu.SemaphoreType.DMA((steps,)),
        ],
        compiler_params=pltpu.CompilerParams(vmem_limit_bytes=6 * MIB),
        cost_estimate=pl.CostEstimate(flops=0, bytes_accessed=4 * 2**20, transcendentals=0),
        name="graft",
    )(own_sums, other_sums, resident(raw))


def renew_kernel(
    place_ref, a_ref, nh_ref, nl_ref, far_ref, out_ref, gh, gl, th, tl
):
    size = a_ref.shape[0]
    half = size // 2
    tiles = size // TILE
    side = place_ref[0]
    used = place_ref[1 + tiles] != 0

    for p in range(tiles):
        for c in range(tiles):
            if p < half // TILE:
                high, low = nh_ref[span(p), span(c)], nl_ref[span(p), span(c)]
            else:
                high, low = split(far_ref[span(p - half // TILE), span(c)])
            for block, target, flipped in ((high, gh, th), (low, gl, tl)):
                target[span(p), span(c)] = block
                flipped[span(c), span(p)] = block.T

    def write(i, j, block):
        rows = pl.ds(pl.multiple_of(i * TILE, TILE), TILE)
        cols = pl.ds(pl.multiple_of(j * TILE, TILE), TILE)
        gain = jnp.where(used, block * ((1.0 - decay_rate) / size), 0.0)
        out_ref[rows, cols] = decay_rate * a_ref[rows, cols] + gain

    def products(lh, ll, rh, rl, where):
        for j in range(tiles):
            low_rows = slice(j * TILE, size)
            column = dot3(lh[low_rows, :], ll[low_rows, :], rh[:, span(j)], rl[:, span(j)])
            for i in range(j, tiles):
                block = column[span(i - j)]
                write(where(i), where(j), block)
                if i != j:
                    write(where(j), where(i), block.T)

    @pl.when(side == 0)
    def _():
        products(gh, gl, th, tl, lambda i: place_ref[1 + i])

    @pl.when(side != 0)
    def _():
        products(th, tl, gh, gl, lambda i: i)


def renew(place, factor, near_high, near_low, far):
    size = factor.shape[0]
    return pl.pallas_call(
        renew_kernel,
        out_shape=jax.ShapeDtypeStruct((size, size), jnp.float32),
        in_specs=[smem()] + [vmem()] * 4,
        out_specs=vmem(),
        scratch_shapes=[pltpu.VMEM((size, size), jnp.bfloat16)] * 4,
        compiler_params=pltpu.CompilerParams(vmem_limit_bytes=56 * MIB),
        cost_estimate=pl.CostEstimate(
            flops=4 * size**3, bytes_accessed=12 * 2**20, transcendentals=0
        ),
        name="renew",
    )(place, factor, near_high, near_low, far)


def per_device(grad, factors, owners):
    row_count = grad.shape[0]
    block_size = factors.shape[-1]
    owner_count = lax.axis_size("block")
    dp_index = lax.axis_index("dp")
    blk_index = lax.axis_index("block")
    side = dp_index % 2
    slot = dp_index // 2
    outer_pair = (dp_index == 0) | (dp_index == 3)
    groups = [
        [x * owner_count + b for x in pair for b in range(owner_count)] for pair in ((0, 3), (1, 2))
    ]

    def exchange(x):
        return lax.all_to_all(
            x, BOTH, split_axis=0, concat_axis=0, tiled=True, axis_index_groups=groups
        )

    def swap(x):
        return lax.ppermute(x, "dp", [(i, i ^ 1) for i in range(4)])

    order = jnp.where(outer_pair, jnp.array([0, 3, 1, 2]), jnp.array([1, 2, 0, 3]))
    used = jnp.sum(owners == blk_index) > slot
    place = jnp.concatenate([side[None], order, used[None]]).astype(jnp.int32)

    near = exchange(deal(owners, grad, owner_count, False)).reshape(block_size // 2, block_size)
    other_grad = swap(grad)
    own_factor = factors[0, 0]
    x_high, x_low, pack = root(own_factor)
    pack, other_grad = lax.optimization_barrier((pack, other_grad))
    other_pack = swap(pack)
    dealt = deal(owners, other_grad, owner_count, True)
    near, dealt = lax.optimization_barrier((near, dealt))
    far = exchange(dealt).reshape(block_size // 2, block_size)

    early, near_high, near_low, near_sum = early_part(place, near, x_high, x_low)
    y_high, y_low, grad_sum = middle_part(place, near_sum, far, early, pack)
    raw, sums = last_part(place, grad_sum, y_high, y_low, other_pack)
    scaled = graft(sums, swap(sums), raw)
    scaled, far = lax.optimization_barrier((scaled, far))
    back = exchange(scaled.reshape(2 * owner_count, row_count, block_size))
    update = collect(owners, back)
    new_own = renew(place, own_factor, near_high, near_low, far)
    return (new_own[None, None], update)


def solution(mesh):
    placed = (P(BOTH, None), P("dp", "block", None, None), P())
    return jax.shard_map(
        per_device,
        mesh=mesh,
        in_specs=placed,
        out_specs=(P("dp", "block", None, None), P(BOTH, None)),
        check_vma=False,
    )
```

```python
import jax
import jax.numpy as jnp
from jax import lax
from jax.experimental import pallas as pl
from jax.experimental.pallas import tpu as pltpu
from jax.sharding import PartitionSpec as P

BOTH = ("dp", "block")
TILE = 256
OUTER_ORDER = (0, 3, 1, 2)
INNER_ORDER = (1, 2, 0, 3)
MIB = 1024 * 1024

decay_rate = 0.9
epsilon = 1e-06


def vmem():
    return pl.BlockSpec(memory_space=pltpu.VMEM)


def anywhere():
    return pl.BlockSpec(memory_space=pl.ANY)


def resident(x):
    return pltpu.with_memory_space_constraint(x, pltpu.VMEM)


def in_hbm(x):
    return pltpu.with_memory_space_constraint(x, pltpu.HBM)


def smem():
    return pl.BlockSpec(memory_space=pltpu.SMEM)


def diag_mask():
    rows = lax.broadcasted_iota(jnp.int32, (TILE, TILE), 0)
    cols = lax.broadcasted_iota(jnp.int32, (TILE, TILE), 1)
    return rows, cols


def span(index):
    return slice(index * TILE, (index + 1) * TILE)


def split(value):
    high = value.astype(jnp.bfloat16)
    low = (value - high.astype(jnp.float32)).astype(jnp.bfloat16)
    return high, low


def dot3(a_high, a_low, b_high, b_low):
    def one(a, b):
        return jnp.dot(a, b, preferred_element_type=jnp.float32)

    return one(a_high, b_high) + (one(a_high, b_low) + one(a_low, b_high))


def put_split(high_ref, low_ref, i, j, block):
    high, low = split(block)
    high_ref[span(i), span(j)] = high
    low_ref[span(i), span(j)] = low


def put_both(high_ref, low_ref, i, j, block):
    put_split(high_ref, low_ref, i, j, block)
    if i != j:
        put_split(high_ref, low_ref, j, i, block.T)


def place_of(owners_ref, count_ref, c):
    owner = owners_ref[c]
    slot = count_ref[owner]
    count_ref[owner] = slot + 1
    return slot * count_ref.shape[0] + owner


def clear(count_ref):
    @pl.loop(0, count_ref.shape[0])
    def _(o):
        count_ref[o] = 0


def deal_kernel(owners_ref, grad_hbm, out_hbm, count_ref, buffer, load_sem, sem):
    load = pltpu.make_async_copy(grad_hbm, buffer, load_sem)
    load.start()
    clear(count_ref)
    load.wait()
    deal_blocks(owners_ref, buffer, out_hbm, count_ref, sem)


def deal_resident_kernel(owners_ref, grad, out_hbm, count_ref, sem):
    clear(count_ref)
    deal_blocks(owners_ref, grad, out_hbm, count_ref, sem)


def deal_blocks(owners_ref, grad, out_hbm, count_ref, sem):
    width = out_hbm.shape[-1]
    for c in range(owners_ref.shape[0]):
        place = place_of(owners_ref, count_ref, c)
        cols = slice(c * width, (c + 1) * width)
        pltpu.make_async_copy(grad.at[:, cols], out_hbm.at[place], sem).start()
    pltpu.make_async_copy(grad, grad, sem).wait()


def collect_kernel(owners_ref, back, out_hbm, count_ref, sem):
    width = back.shape[-1]
    clear(count_ref)
    for c in range(owners_ref.shape[0]):
        place = place_of(owners_ref, count_ref, c)
        cols = slice(c * width, (c + 1) * width)
        pltpu.make_async_copy(back.at[place], out_hbm.at[:, cols], sem).start()
    pltpu.make_async_copy(out_hbm, out_hbm, sem).wait()


def deal(owners, grad, owner_count, landed):
    rows = grad.shape[0]
    count = owners.shape[0]
    width = grad.shape[1] // count
    counts, sem = pltpu.SMEM((owner_count,), jnp.int32), pltpu.SemaphoreType.DMA(())
    buffers = [pltpu.VMEM(grad.shape, jnp.float32), sem, sem]
    return pl.pallas_call(
        deal_resident_kernel if landed else deal_kernel,
        out_shape=pltpu.HBM((2 * owner_count, rows, width), jnp.float32),
        in_specs=[smem(), vmem() if landed else anywhere()],
        out_specs=anywhere(),
        scratch_shapes=[counts, sem] if landed else [counts] + buffers,
        compiler_params=pltpu.CompilerParams(vmem_limit_bytes=16 * MIB),
        cost_estimate=pl.CostEstimate(flops=5 * 10**10, bytes_accessed=2**22, transcendentals=0),
        name="deal",
    )(owners, resident(grad) if landed else in_hbm(grad))


def collect(owners, back):
    places, rows, width = back.shape
    return pl.pallas_call(
        collect_kernel,
        out_shape=jax.ShapeDtypeStruct((rows, owners.shape[0] * width), jnp.float32),
        in_specs=[smem(), vmem()],
        out_specs=anywhere(),
        scratch_shapes=[
            pltpu.SMEM((places // 2,), jnp.int32),
            pltpu.SemaphoreType.DMA(()),
        ],
        compiler_params=pltpu.CompilerParams(vmem_limit_bytes=16 * MIB),
        cost_estimate=pl.CostEstimate(flops=0, bytes_accessed=2**22, transcendentals=0),
        name="collect",
    )(owners, resident(back))


def lower_blocks(tiles):
    return [(i, j) for j in range(tiles) for i in range(j + 1, tiles)]


def root_kernel(
    a_hbm, xh_hbm, xl_hbm, pack_hbm,
    a, sh, sl, s2, s2h, s2l, s3h, s3l, qh, ql, xh, xl, pack, in_sems, out_sems,
):
    size = a.shape[0]
    tiles = size // TILE
    rows, cols = diag_mask()
    on_diag = rows == cols
    loads = [
        pltpu.make_async_copy(a_hbm.at[span(b)], a.at[span(b)], in_sems.at[b]) for b in range(tiles)
    ]
    for load in loads:
        load.start()
    diagonal = jnp.zeros((8, TILE), jnp.float32)
    for b in range(tiles):
        loads[b].wait()
        block = jnp.where(on_diag, a[span(b), span(b)], 0.0)
        diagonal += jnp.sum(block.reshape(TILE // 8, 8, TILE), axis=0)
    shrink = 0.25 / (2.0 * jnp.sum(diagonal) / size)

    def step_block(i, j):
        block = a[span(i), span(j)] * -shrink
        if i == j:
            block = jnp.where(on_diag, 1.25 + block, block)
        return block

    for i in range(tiles):
        for j in range(tiles):
            put_split(sh, sl, i, j, step_block(i, j))

    def product(ah, al, bh, bl, j):
        low_rows = slice(j * TILE, size)
        return dot3(ah[low_rows, :], al[low_rows, :], bh[:, span(j)], bl[:, span(j)])

    for j in range(tiles):
        column = product(sh, sl, sh, sl, j)
        s2[j * TILE :, span(j)] = column
        for i in range(j, tiles):
            put_both(s2h, s2l, i, j, column[span(i - j)])
    for j in range(tiles):
        column = product(sh, sl, s2h, s2l, j)
        for i in range(j, tiles):
            block = column[span(i - j)]
            put_both(s3h, s3l, i, j, block)
            put_both(qh, ql, i, j, block - 1.25 * s2[span(i), span(j)])

    stores = []

    def store(source, target, where):
        k = len(stores)
        stores.append(pltpu.make_async_copy(source.at[where], target.at[where], out_sems.at[k]))
        stores[-1].start()

    offset = len(lower_blocks(tiles))
    last = (offset + tiles // 2) * TILE
    for j in range(tiles):
        column = product(s3h, s3l, qh, ql, j)
        for i in range(j, tiles):
            block = column[span(i - j)] + 1.25 * step_block(i, j)
            put_both(xh, xl, i, j, block)
            if i != j:
                pack[span(lower_blocks(tiles).index((i, j)))] = block
            else:
                s2[span(i), span(i)] = block
        if j + 1 < tiles:
            first = lower_blocks(tiles).index((j + 1, j))
            store(pack, pack_hbm, slice(first * TILE, (first + tiles - 1 - j) * TILE))
        if j % 2:
            first, second = s2[span(j - 1), span(j - 1)], s2[span(j), span(j)]
            pack[span(offset + j // 2)] = jnp.where(rows >= cols, first, second)
            line = jnp.sum(jnp.where(on_diag, second, 0.0), axis=0, keepdims=True)
            start = last + j // 2 * 8
            pack[start : start + 8] = jnp.broadcast_to(line, (8, TILE))
            store(pack, pack_hbm, span(offset + j // 2))
            store(pack, pack_hbm, slice(start, start + 8))
        store(xh, xh_hbm, span(j))
        store(xl, xl_hbm, span(j))
    for copy in stores:
        copy.wait()


def packed_rows(size):
    tiles = size // TILE
    return (len(lower_blocks(tiles)) + tiles // 2) * TILE + 8 * (tiles // 2)


def root(factor):
    size = factor.shape[0]
    tiles = size // TILE
    half = pltpu.HBM((size, size), jnp.bfloat16)
    square = pltpu.VMEM((size, size), jnp.float32)
    square_half = pltpu.VMEM((size, size), jnp.bfloat16)
    packed = (packed_rows(size), TILE)
    return pl.pallas_call(
        root_kernel,
        out_shape=[half, half, pltpu.HBM(packed, jnp.float32)],
        in_specs=[anywhere()],
        out_specs=[anywhere()] * 3,
        scratch_shapes=[square, square_half, square_half, square]
        + [square_half] * 8
        + [
            pltpu.VMEM(packed, jnp.float32),
            pltpu.SemaphoreType.DMA((tiles,)),
            pltpu.SemaphoreType.DMA((4 * tiles - 1,)),
        ],
        compiler_params=pltpu.CompilerParams(vmem_limit_bytes=44 * MIB),
        cost_estimate=pl.CostEstimate(flops=0, bytes_accessed=0, transcendentals=0),
        name="root",
    )(in_hbm(factor))


def unpack_block(pack_ref, tiles, i, j, rows, cols):
    if i != j:
        return pack_ref[span(lower_blocks(tiles).index((i, j)))]
    offset = len(lower_blocks(tiles))
    last = (offset + tiles // 2) * TILE
    both = pack_ref[span(offset + i // 2)]
    if i % 2 == 0:
        return jnp.where(rows >= cols, both, both.T)
    diagonal = pack_ref[last + (i // 2) * 8 : last + (i // 2) * 8 + 1]
    return jnp.where(rows == cols, diagonal, jnp.where(rows < cols, both, both.T))


def unpack_column(pack_ref, tiles, j, high_ref, low_ref):
    rows, cols = diag_mask()
    for i in range(j, tiles):
        put_both(high_ref, low_ref, i, j, unpack_block(pack_ref, tiles, i, j, rows, cols))


def unpack_left(place_ref, pack_ref, tiles, parts, high_ref, low_ref):
    rows, cols = diag_mask()

    def by_order(order):
        for r in range(tiles // 2):
            for c in range(*parts):
                i, j = order[r], order[c]
                block = unpack_block(pack_ref, tiles, max(i, j), min(i, j), rows, cols)
                put_split(high_ref, low_ref, r, c - parts[0], block if i >= j else block.T)

    pl.when(place_ref[1] == 0)(lambda: by_order(OUTER_ORDER))
    pl.when(place_ref[1] != 0)(lambda: by_order(INNER_ORDER))


def squares(block):
    return jnp.sum((block * block).reshape(block.shape[0] // 8, 8, TILE), axis=0)


def place_left(place_ref, parts, tiles, high_ref, low_ref, lh, ll):
    for r in range(tiles // 2):
        source_rows = pl.ds(pl.multiple_of(place_ref[1 + r] * TILE, TILE), TILE)
        for c in range(parts[0], parts[1]):
            source_cols = pl.ds(pl.multiple_of(place_ref[1 + c] * TILE, TILE), TILE)
            lh[span(r), span(c - parts[0])] = high_ref[source_rows, source_cols]
            ll[span(r), span(c - parts[0])] = low_ref[source_rows, source_cols]


def early_kernel(place_ref, near, xh, xl, out, nh, nl, sum_ref, lh, ll):
    half, size = near.shape
    tiles = size // TILE
    side = place_ref[0]
    total = jnp.zeros((8, TILE), jnp.float32)
    for j in range(tiles):
        block = near[:, span(j)]
        nh[:, span(j)], nl[:, span(j)] = split(block)
        total += squares(block)
    sum_ref[...] = jnp.full(sum_ref.shape, jnp.sum(total), jnp.float32)

    @pl.when(side == 0)
    def _():
        place_left(place_ref, (0, tiles // 2), tiles, xh, xl, lh, ll)
        for j in range(tiles):
            out[:, span(j)] = dot3(lh[...], ll[...], nh[:, span(j)], nl[:, span(j)])

    @pl.when(side != 0)
    def _():
        for j in range(tiles):
            out[:, span(j)] = dot3(nh[...], nl[...], xh[:, span(j)], xl[:, span(j)])


def early_part(place, near, x_high, x_low):
    half, size = near.shape
    square = pltpu.VMEM((half, half), jnp.bfloat16)
    rows = pltpu.HBM((half, size), jnp.bfloat16)
    return pl.pallas_call(
        early_kernel,
        out_shape=[
            pltpu.HBM((half, size), jnp.float32), rows, rows,
            pltpu.HBM((8, 128), jnp.float32),
        ],
        in_specs=[smem()] + [vmem()] * 3,
        out_specs=[vmem()] * 4,
        scratch_shapes=[square, square],
        compiler_params=pltpu.CompilerParams(vmem_limit_bytes=56 * MIB),
        cost_estimate=pl.CostEstimate(flops=0, bytes_accessed=0, transcendentals=0),
        name="early_part",
    )(place, in_hbm(near), in_hbm(x_high), in_hbm(x_low))


def middle_kernel(
    place_ref, near_sum_hbm, far, early_hbm, pack_hbm, yh, yl, sum_ref,
    near_sum, early, pack, xh, xl, fh, fl, lh, ll, sems,
):
    half, size = far.shape
    tiles = size // TILE
    side = place_ref[0]
    pack_load = pltpu.make_async_copy(pack_hbm, pack, sems.at[0])
    early_load = pltpu.make_async_copy(early_hbm, early, sems.at[1])
    sum_load = pltpu.make_async_copy(near_sum_hbm, near_sum, sems.at[2])
    for load in (pack_load, early_load, sum_load):
        load.start()
    total = jnp.zeros((8, TILE), jnp.float32)
    for j in range(tiles):
        block = far[:, span(j)]
        fh[:, span(j)], fl[:, span(j)] = split(block)
        total += squares(block)
    for load in (pack_load, early_load, sum_load):
        load.wait()
    sum_ref[...] = near_sum[...] + jnp.sum(total)

    @pl.when(side == 0)
    def _():
        unpack_left(place_ref, pack, tiles, (tiles // 2, tiles), lh, ll)
        for j in range(tiles):
            column = early[:, span(j)] + dot3(lh[...], ll[...], fh[:, span(j)], fl[:, span(j)])
            yh[:half, span(j)], yl[:half, span(j)] = split(column)

    @pl.when(side != 0)
    def _():
        for j in range(tiles):
            unpack_column(pack, tiles, j, xh, xl)
            yh[:half, span(j)], yl[:half, span(j)] = split(early[:, span(j)])
            column = dot3(fh[...], fl[...], xh[:, span(j)], xl[:, span(j)])
            yh[half:, span(j)], yl[half:, span(j)] = split(column)


def middle_part(place, near_sum, far, early, pack):
    half, size = far.shape
    wide = pltpu.VMEM((half, size), jnp.bfloat16)
    square = pltpu.VMEM((half, half), jnp.bfloat16)
    big = pltpu.VMEM((size, size), jnp.bfloat16)
    return pl.pallas_call(
        middle_kernel,
        out_shape=[big, big, jax.ShapeDtypeStruct((8, 128), jnp.float32)],
        in_specs=[smem(), anywhere(), vmem(), anywhere(), anywhere()],
        out_specs=[vmem()] * 3,
        scratch_shapes=[
            pltpu.VMEM(near_sum.shape, jnp.float32),
            pltpu.VMEM((half, size), jnp.float32),
            pltpu.VMEM(pack.shape, jnp.float32),
            big, big, wide, wide, square, square,
            pltpu.SemaphoreType.DMA((3,)),
        ],
        compiler_params=pltpu.CompilerParams(vmem_limit_bytes=24 * MIB),
        cost_estimate=pl.CostEstimate(flops=0, bytes_accessed=0, transcendentals=0),
        name="middle_part",
    )(place, in_hbm(near_sum), resident(far), in_hbm(early), in_hbm(pack))


def last_kernel(place_ref, grad_sum_ref, yh, yl, pack, raw, sums_ref, ph, pw, lh, ll):
    half, size = raw.shape
    tiles = size // TILE
    side = place_ref[0]

    def multiply(ah, al, bh, bl, prepare):
        total = jnp.zeros((8, TILE), jnp.float32)
        for j in range(tiles):
            prepare(j)
            column = dot3(ah, al, bh[:, span(j)], bl[:, span(j)])
            raw[:, span(j)] = column
            total += squares(column)
        lane = lax.broadcasted_iota(jnp.int32, (8, 128), 1)
        sums_ref[...] = jnp.where(lane == 0, jnp.sum(total), grad_sum_ref[...])

    @pl.when(side == 0)
    def _():
        multiply(yh[:half], yl[:half], ph, pw, lambda j: unpack_column(pack, tiles, j, ph, pw))

    @pl.when(side != 0)
    def _():
        unpack_left(place_ref, pack, tiles, (0, tiles), lh, ll)
        multiply(lh[...], ll[...], yh, yl, lambda j: None)


def last_part(place, grad_sum, y_high, y_low, pack):
    size = y_high.shape[0]
    half = size // 2
    wide = pltpu.VMEM((half, size), jnp.bfloat16)
    big = pltpu.VMEM((size, size), jnp.bfloat16)
    return pl.pallas_call(
        last_kernel,
        out_shape=[
            pltpu.VMEM((half, size), jnp.float32),
            jax.ShapeDtypeStruct((8, 128), jnp.float32),
        ],
        in_specs=[smem()] + [vmem()] * 4,
        out_specs=[vmem(), vmem()],
        scratch_shapes=[big, big, wide, wide],
        compiler_params=pltpu.CompilerParams(vmem_limit_bytes=32 * MIB),
        cost_estimate=pl.CostEstimate(
            flops=3 * size**3, bytes_accessed=12 * 2**20, transcendentals=0
        ),
        name="last_part",
    )(place, grad_sum, resident(y_high), resident(y_low), resident(pack))


def graft_kernel(own_ref, other_ref, raw, out_hbm, buffer, sems):
    half, size = buffer.shape
    steps = sems.shape[0]
    count = size * size
    own = own_ref[...]
    raw_sum = own[:1, :1] + other_ref[:1, :1]
    grad_sum = own[:1, 1:2]
    scale = jnp.sqrt(grad_sum / count + epsilon) / jnp.sqrt(raw_sum / count + epsilon)
    stores = []
    for k in range(steps):
        rows = slice(k * half // steps, (k + 1) * half // steps)
        buffer[rows] = raw[rows] * scale
        stores.append(pltpu.make_async_copy(buffer.at[rows], out_hbm.at[rows], sems.at[k]))
        stores[-1].start()
    for store in stores:
        store.wait()


def graft(own_sums, other_sums, raw):
    steps = 4
    return pl.pallas_call(
        graft_kernel,
        out_shape=pltpu.HBM(raw.shape, jnp.float32),
        in_specs=[vmem(), vmem(), vmem()],
        out_specs=anywhere(),
        scratch_shapes=[
            pltpu.VMEM(raw.shape, jnp.float32),
            pltpu.SemaphoreType.DMA((steps,)),
        ],
        compiler_params=pltpu.CompilerParams(vmem_limit_bytes=6 * MIB),
        cost_estimate=pl.CostEstimate(flops=0, bytes_accessed=4 * 2**20, transcendentals=0),
        name="graft",
    )(own_sums, other_sums, resident(raw))


def renew_kernel(place_ref, a_ref, nh_ref, nl_ref, far_ref, out_ref, high_ref, low_ref):
    size = a_ref.shape[0]
    half = size // 2
    tiles = size // TILE
    side = place_ref[0]
    used = place_ref[1 + tiles] != 0

    for p in range(tiles):
        for c in range(tiles):
            if p < half // TILE:
                high, low = nh_ref[span(p), span(c)], nl_ref[span(p), span(c)]
            else:
                high, low = split(far_ref[span(p - half // TILE), span(c)])
            for block, target in ((high, high_ref), (low, low_ref)):
                target[side, span(p), span(c)] = block
                target[1 - side, span(c), span(p)] = block.T

    def write(i, j, block):
        i, j = (jnp.where(side == 0, place_ref[1 + k], k) for k in (i, j))
        rows = pl.ds(pl.multiple_of(i * TILE, TILE), TILE)
        cols = pl.ds(pl.multiple_of(j * TILE, TILE), TILE)
        gain = jnp.where(used, block * ((1.0 - decay_rate) / size), 0.0)
        out_ref[rows, cols] = decay_rate * a_ref[rows, cols] + gain

    for j in range(tiles):
        low_rows = slice(j * TILE, size)
        column = dot3(
            high_ref[0, low_rows, :], low_ref[0, low_rows, :],
            high_ref[1, :, span(j)], low_ref[1, :, span(j)],
        )
        for i in range(j, tiles):
            block = column[span(i - j)]
            write(i, j, block)
            if i != j:
                write(j, i, block.T)


def renew(place, factor, near_high, near_low, far):
    size = factor.shape[0]
    return pl.pallas_call(
        renew_kernel,
        out_shape=jax.ShapeDtypeStruct((size, size), jnp.float32),
        in_specs=[smem()] + [vmem()] * 4,
        out_specs=vmem(),
        scratch_shapes=[pltpu.VMEM((2, size, size), jnp.bfloat16)] * 2,
        compiler_params=pltpu.CompilerParams(vmem_limit_bytes=56 * MIB),
        cost_estimate=pl.CostEstimate(
            flops=4 * size**3, bytes_accessed=12 * 2**20, transcendentals=0
        ),
        name="renew",
    )(place, factor, near_high, near_low, far)


def per_device(grad, factors, owners):
    row_count = grad.shape[0]
    block_size = factors.shape[-1]
    owner_count = lax.axis_size("block")
    dp_index = lax.axis_index("dp")
    blk_index = lax.axis_index("block")
    side = dp_index % 2
    slot = dp_index // 2
    outer_pair = (dp_index == 0) | (dp_index == 3)
    groups = [
        [x * owner_count + b for x in pair for b in range(owner_count)] for pair in ((0, 3), (1, 2))
    ]

    def exchange(x):
        return lax.all_to_all(
            x, BOTH, split_axis=0, concat_axis=0, tiled=True, axis_index_groups=groups
        )

    def swap(x):
        return lax.ppermute(x, "dp", [(i, i ^ 1) for i in range(4)])

    order = jnp.where(outer_pair, jnp.array(OUTER_ORDER), jnp.array(INNER_ORDER))
    used = jnp.sum(owners == blk_index) > slot
    place = jnp.concatenate([side[None], order, used[None]]).astype(jnp.int32)

    near = exchange(deal(owners, grad, owner_count, False)).reshape(block_size // 2, block_size)
    other_grad = swap(grad)
    own_factor = factors[0, 0]
    x_high, x_low, pack = root(own_factor)
    pack, other_grad = lax.optimization_barrier((pack, other_grad))
    other_pack = swap(pack)
    dealt = deal(owners, other_grad, owner_count, True)
    near, dealt = lax.optimization_barrier((near, dealt))
    far = exchange(dealt).reshape(block_size // 2, block_size)

    early, near_high, near_low, near_sum = early_part(place, near, x_high, x_low)
    y_high, y_low, grad_sum = middle_part(place, near_sum, far, early, pack)
    raw, sums = last_part(place, grad_sum, y_high, y_low, other_pack)
    scaled = graft(sums, swap(sums), raw)
    scaled, far = lax.optimization_barrier((scaled, far))
    back = exchange(scaled.reshape(2 * owner_count, row_count, block_size))
    update = collect(owners, back)
    new_own = renew(place, own_factor, near_high, near_low, far)
    return (new_own[None, None], update)


def solution(mesh):
    placed = (P(BOTH, None), P("dp", "block", None, None), P())
    return jax.shard_map(
        per_device,
        mesh=mesh,
        in_specs=placed,
        out_specs=(P("dp", "block", None, None), P(BOTH, None)),
        check_vma=False,
    )
```

```python
import jax
import jax.numpy as jnp
from jax import lax
from jax.experimental import pallas as pl
from jax.experimental.pallas import tpu as pltpu
from jax.sharding import PartitionSpec as P

BOTH = ("dp", "block")
TILE = 256
OUTER_ORDER = (0, 3, 1, 2)
INNER_ORDER = (1, 2, 0, 3)
MIB = 1024 * 1024

decay_rate = 0.9
epsilon = 1e-06


def vmem():
    return pl.BlockSpec(memory_space=pltpu.VMEM)


def anywhere():
    return pl.BlockSpec(memory_space=pl.ANY)


def resident(x):
    return pltpu.with_memory_space_constraint(x, pltpu.VMEM)


def in_hbm(x):
    return pltpu.with_memory_space_constraint(x, pltpu.HBM)


def smem():
    return pl.BlockSpec(memory_space=pltpu.SMEM)


def diag_mask():
    rows = lax.broadcasted_iota(jnp.int32, (TILE, TILE), 0)
    cols = lax.broadcasted_iota(jnp.int32, (TILE, TILE), 1)
    return rows, cols


def span(index):
    return slice(index * TILE, (index + 1) * TILE)


def split(value):
    high = value.astype(jnp.bfloat16)
    low = (value - high.astype(jnp.float32)).astype(jnp.bfloat16)
    return high, low


def dot3(a_high, a_low, b_high, b_low):
    def one(a, b):
        return jnp.dot(a, b, preferred_element_type=jnp.float32)

    return one(a_high, b_high) + (one(a_high, b_low) + one(a_low, b_high))


def put_split(high_ref, low_ref, i, j, block):
    high, low = split(block)
    high_ref[span(i), span(j)] = high
    low_ref[span(i), span(j)] = low


def put_both(high_ref, low_ref, i, j, block):
    put_split(high_ref, low_ref, i, j, block)
    if i != j:
        put_split(high_ref, low_ref, j, i, block.T)


def place_of(owners_ref, count_ref, c):
    owner = owners_ref[c]
    slot = count_ref[owner]
    count_ref[owner] = slot + 1
    return slot * count_ref.shape[0] + owner


def clear(count_ref):
    @pl.loop(0, count_ref.shape[0])
    def _(o):
        count_ref[o] = 0


def deal_kernel(owners_ref, grad_hbm, out_hbm, count_ref, buffer, load_sem, sem):
    load = pltpu.make_async_copy(grad_hbm, buffer, load_sem)
    load.start()
    clear(count_ref)
    load.wait()
    deal_blocks(owners_ref, buffer, out_hbm, count_ref, sem)


def deal_resident_kernel(owners_ref, grad, out_hbm, count_ref, sem):
    clear(count_ref)
    deal_blocks(owners_ref, grad, out_hbm, count_ref, sem)


def deal_blocks(owners_ref, grad, out_hbm, count_ref, sem):
    width = out_hbm.shape[-1]
    for c in range(owners_ref.shape[0]):
        place = place_of(owners_ref, count_ref, c)
        cols = slice(c * width, (c + 1) * width)
        pltpu.make_async_copy(grad.at[:, cols], out_hbm.at[place], sem).start()
    pltpu.make_async_copy(grad, grad, sem).wait()


def collect_kernel(owners_ref, back, out_hbm, count_ref, sem):
    width = back.shape[-1]
    clear(count_ref)
    for c in range(owners_ref.shape[0]):
        place = place_of(owners_ref, count_ref, c)
        cols = slice(c * width, (c + 1) * width)
        pltpu.make_async_copy(back.at[place], out_hbm.at[:, cols], sem).start()
    pltpu.make_async_copy(out_hbm, out_hbm, sem).wait()


def deal(owners, grad, owner_count, landed):
    rows = grad.shape[0]
    count = owners.shape[0]
    width = grad.shape[1] // count
    counts, sem = pltpu.SMEM((owner_count,), jnp.int32), pltpu.SemaphoreType.DMA(())
    buffers = [pltpu.VMEM(grad.shape, jnp.float32), sem, sem]
    return pl.pallas_call(
        deal_resident_kernel if landed else deal_kernel,
        out_shape=pltpu.HBM((2 * owner_count, rows, width), jnp.float32),
        in_specs=[smem(), vmem() if landed else anywhere()],
        out_specs=anywhere(),
        scratch_shapes=[counts, sem] if landed else [counts] + buffers,
        compiler_params=pltpu.CompilerParams(vmem_limit_bytes=16 * MIB),
        cost_estimate=pl.CostEstimate(flops=5 * 10**10, bytes_accessed=2**22, transcendentals=0),
        name="deal",
    )(owners if landed else in_hbm(owners), resident(grad) if landed else in_hbm(grad))


def collect(owners, back):
    places, rows, width = back.shape
    return pl.pallas_call(
        collect_kernel,
        out_shape=jax.ShapeDtypeStruct((rows, owners.shape[0] * width), jnp.float32),
        in_specs=[smem(), vmem()],
        out_specs=anywhere(),
        scratch_shapes=[
            pltpu.SMEM((places // 2,), jnp.int32),
            pltpu.SemaphoreType.DMA(()),
        ],
        compiler_params=pltpu.CompilerParams(vmem_limit_bytes=16 * MIB),
        cost_estimate=pl.CostEstimate(flops=0, bytes_accessed=2**22, transcendentals=0),
        name="collect",
    )(owners, resident(back))


def lower_blocks(tiles):
    return [(i, j) for j in range(tiles) for i in range(j + 1, tiles)]


def root_kernel(
    a_hbm, xh_hbm, xl_hbm, pack_hbm,
    a, sh, sl, s2, s2h, s2l, s3h, s3l, qh, ql, xh, xl, pack, in_sems, out_sems,
):
    size = a.shape[0]
    tiles = size // TILE
    rows, cols = diag_mask()
    on_diag = rows == cols
    loads = [
        pltpu.make_async_copy(a_hbm.at[span(b)], a.at[span(b)], in_sems.at[b]) for b in range(tiles)
    ]
    for load in loads:
        load.start()
    diagonal = jnp.zeros((8, TILE), jnp.float32)
    for b in range(tiles):
        loads[b].wait()
        block = jnp.where(on_diag, a[span(b), span(b)], 0.0)
        diagonal += jnp.sum(block.reshape(TILE // 8, 8, TILE), axis=0)
    shrink = 0.25 / (2.0 * jnp.sum(diagonal) / size)

    def step_block(i, j):
        block = a[span(i), span(j)] * -shrink
        if i == j:
            block = jnp.where(on_diag, 1.25 + block, block)
        return block

    for i in range(tiles):
        for j in range(tiles):
            put_split(sh, sl, i, j, step_block(i, j))

    def product(ah, al, bh, bl, j):
        low_rows = slice(j * TILE, size)
        return dot3(ah[low_rows, :], al[low_rows, :], bh[:, span(j)], bl[:, span(j)])

    for j in range(tiles):
        column = product(sh, sl, sh, sl, j)
        s2[j * TILE :, span(j)] = column
        for i in range(j, tiles):
            put_both(s2h, s2l, i, j, column[span(i - j)])
    for j in range(tiles):
        column = product(sh, sl, s2h, s2l, j)
        for i in range(j, tiles):
            block = column[span(i - j)]
            put_both(s3h, s3l, i, j, block)
            put_both(qh, ql, i, j, block - 1.25 * s2[span(i), span(j)])

    stores = []

    def store(source, target, where):
        k = len(stores)
        stores.append(pltpu.make_async_copy(source.at[where], target.at[where], out_sems.at[k]))
        stores[-1].start()

    offset = len(lower_blocks(tiles))
    last = (offset + tiles // 2) * TILE
    for j in range(tiles):
        column = product(s3h, s3l, qh, ql, j)
        for i in range(j, tiles):
            block = column[span(i - j)] + 1.25 * step_block(i, j)
            put_both(xh, xl, i, j, block)
            if i != j:
                pack[span(lower_blocks(tiles).index((i, j)))] = block
            else:
                s2[span(i), span(i)] = block
        if j + 1 < tiles:
            first = lower_blocks(tiles).index((j + 1, j))
            store(pack, pack_hbm, slice(first * TILE, (first + tiles - 1 - j) * TILE))
        if j % 2:
            first, second = s2[span(j - 1), span(j - 1)], s2[span(j), span(j)]
            pack[span(offset + j // 2)] = jnp.where(rows >= cols, first, second)
            line = jnp.sum(jnp.where(on_diag, second, 0.0), axis=0, keepdims=True)
            start = last + j // 2 * 8
            pack[start : start + 8] = jnp.broadcast_to(line, (8, TILE))
            store(pack, pack_hbm, span(offset + j // 2))
            store(pack, pack_hbm, slice(start, start + 8))
        store(xh, xh_hbm, span(j))
        store(xl, xl_hbm, span(j))
    for copy in stores:
        copy.wait()


def packed_rows(size):
    tiles = size // TILE
    return (len(lower_blocks(tiles)) + tiles // 2) * TILE + 8 * (tiles // 2)


def root(factor):
    size = factor.shape[0]
    tiles = size // TILE
    half = pltpu.HBM((size, size), jnp.bfloat16)
    square = pltpu.VMEM((size, size), jnp.float32)
    square_half = pltpu.VMEM((size, size), jnp.bfloat16)
    packed = (packed_rows(size), TILE)
    return pl.pallas_call(
        root_kernel,
        out_shape=[half, half, pltpu.HBM(packed, jnp.float32)],
        in_specs=[anywhere()],
        out_specs=[anywhere()] * 3,
        scratch_shapes=[square, square_half, square_half, square]
        + [square_half] * 8
        + [
            pltpu.VMEM(packed, jnp.float32),
            pltpu.SemaphoreType.DMA((tiles,)),
            pltpu.SemaphoreType.DMA((4 * tiles - 1,)),
        ],
        compiler_params=pltpu.CompilerParams(vmem_limit_bytes=44 * MIB),
        cost_estimate=pl.CostEstimate(flops=0, bytes_accessed=0, transcendentals=0),
        name="root",
    )(in_hbm(factor))


def unpack_block(pack_ref, tiles, i, j, rows, cols):
    if i != j:
        return pack_ref[span(lower_blocks(tiles).index((i, j)))]
    offset = len(lower_blocks(tiles))
    last = (offset + tiles // 2) * TILE
    both = pack_ref[span(offset + i // 2)]
    if i % 2 == 0:
        return jnp.where(rows >= cols, both, both.T)
    diagonal = pack_ref[last + (i // 2) * 8 : last + (i // 2) * 8 + 1]
    return jnp.where(rows == cols, diagonal, jnp.where(rows < cols, both, both.T))


def unpack_column(pack_ref, tiles, j, high_ref, low_ref):
    rows, cols = diag_mask()
    for i in range(j, tiles):
        put_both(high_ref, low_ref, i, j, unpack_block(pack_ref, tiles, i, j, rows, cols))


def unpack_left(place_ref, pack_ref, tiles, parts, high_ref, low_ref):
    rows, cols = diag_mask()

    def by_order(order):
        for r in range(tiles // 2):
            for c in range(*parts):
                i, j = order[r], order[c]
                block = unpack_block(pack_ref, tiles, max(i, j), min(i, j), rows, cols)
                put_split(high_ref, low_ref, r, c - parts[0], block if i >= j else block.T)

    pl.when(place_ref[1] == 0)(lambda: by_order(OUTER_ORDER))
    pl.when(place_ref[1] != 0)(lambda: by_order(INNER_ORDER))


def squares(block):
    return jnp.sum((block * block).reshape(block.shape[0] // 8, 8, TILE), axis=0)


def place_left(place_ref, parts, tiles, high_ref, low_ref, lh, ll):
    for r in range(tiles // 2):
        source_rows = pl.ds(pl.multiple_of(place_ref[1 + r] * TILE, TILE), TILE)
        for c in range(parts[0], parts[1]):
            source_cols = pl.ds(pl.multiple_of(place_ref[1 + c] * TILE, TILE), TILE)
            lh[span(r), span(c - parts[0])] = high_ref[source_rows, source_cols]
            ll[span(r), span(c - parts[0])] = low_ref[source_rows, source_cols]


def early_kernel(place_ref, near, xh, xl, out, nh, nl, sum_ref, lh, ll):
    half, size = near.shape
    tiles = size // TILE
    side = place_ref[0]
    total = jnp.zeros((8, TILE), jnp.float32)
    for j in range(tiles):
        block = near[:, span(j)]
        nh[:, span(j)], nl[:, span(j)] = split(block)
        total += squares(block)
    sum_ref[...] = jnp.full(sum_ref.shape, jnp.sum(total), jnp.float32)

    @pl.when(side == 0)
    def _():
        place_left(place_ref, (0, tiles // 2), tiles, xh, xl, lh, ll)
        for j in range(tiles):
            out[:, span(j)] = dot3(lh[...], ll[...], nh[:, span(j)], nl[:, span(j)])

    @pl.when(side != 0)
    def _():
        for j in range(tiles):
            out[:, span(j)] = dot3(nh[...], nl[...], xh[:, span(j)], xl[:, span(j)])


def early_part(place, near, x_high, x_low):
    half, size = near.shape
    square = pltpu.VMEM((half, half), jnp.bfloat16)
    rows = pltpu.HBM((half, size), jnp.bfloat16)
    return pl.pallas_call(
        early_kernel,
        out_shape=[
            pltpu.HBM((half, size), jnp.float32), rows, rows,
            pltpu.HBM((8, 128), jnp.float32),
        ],
        in_specs=[smem()] + [vmem()] * 3,
        out_specs=[vmem()] * 4,
        scratch_shapes=[square, square],
        compiler_params=pltpu.CompilerParams(vmem_limit_bytes=56 * MIB),
        cost_estimate=pl.CostEstimate(flops=0, bytes_accessed=0, transcendentals=0),
        name="early_part",
    )(place, in_hbm(near), in_hbm(x_high), in_hbm(x_low))


def middle_kernel(
    place_ref, near_sum_hbm, far, early_hbm, pack_hbm, yh, yl, sum_ref,
    near_sum, early, pack, xh, xl, fh, fl, lh, ll, sems,
):
    half, size = far.shape
    tiles = size // TILE
    side = place_ref[0]
    pack_load = pltpu.make_async_copy(pack_hbm, pack, sems.at[0])
    early_load = pltpu.make_async_copy(early_hbm, early, sems.at[1])
    sum_load = pltpu.make_async_copy(near_sum_hbm, near_sum, sems.at[2])
    for load in (pack_load, early_load, sum_load):
        load.start()
    total = jnp.zeros((8, TILE), jnp.float32)
    for j in range(tiles):
        block = far[:, span(j)]
        fh[:, span(j)], fl[:, span(j)] = split(block)
        total += squares(block)
    for load in (pack_load, sum_load):
        load.wait()
    sum_ref[...] = near_sum[...] + jnp.sum(total)

    @pl.when(side == 0)
    def _():
        unpack_left(place_ref, pack, tiles, (tiles // 2, tiles), lh, ll)
        early_load.wait()
        for j in range(tiles):
            column = early[:, span(j)] + dot3(lh[...], ll[...], fh[:, span(j)], fl[:, span(j)])
            yh[:half, span(j)], yl[:half, span(j)] = split(column)

    @pl.when(side != 0)
    def _():
        for j in range(tiles):
            unpack_column(pack, tiles, j, xh, xl)
            column = dot3(fh[...], fl[...], xh[:, span(j)], xl[:, span(j)])
            yh[half:, span(j)], yl[half:, span(j)] = split(column)
        early_load.wait()
        for j in range(tiles):
            yh[:half, span(j)], yl[:half, span(j)] = split(early[:, span(j)])


def middle_part(place, near_sum, far, early, pack):
    half, size = far.shape
    wide = pltpu.VMEM((half, size), jnp.bfloat16)
    square = pltpu.VMEM((half, half), jnp.bfloat16)
    big = pltpu.VMEM((size, size), jnp.bfloat16)
    return pl.pallas_call(
        middle_kernel,
        out_shape=[big, big, jax.ShapeDtypeStruct((8, 128), jnp.float32)],
        in_specs=[smem(), anywhere(), vmem(), anywhere(), anywhere()],
        out_specs=[vmem()] * 3,
        scratch_shapes=[
            pltpu.VMEM(near_sum.shape, jnp.float32),
            pltpu.VMEM((half, size), jnp.float32),
            pltpu.VMEM(pack.shape, jnp.float32),
            big, big, wide, wide, square, square,
            pltpu.SemaphoreType.DMA((3,)),
        ],
        compiler_params=pltpu.CompilerParams(vmem_limit_bytes=24 * MIB),
        cost_estimate=pl.CostEstimate(flops=0, bytes_accessed=0, transcendentals=0),
        name="middle_part",
    )(place, in_hbm(near_sum), resident(far), in_hbm(early), in_hbm(pack))


def last_kernel(place_ref, grad_sum_ref, yh, yl, pack, raw, sums_ref, ph, pw, lh, ll):
    half, size = raw.shape
    tiles = size // TILE
    side = place_ref[0]

    def multiply(ah, al, bh, bl, prepare):
        total = jnp.zeros((8, TILE), jnp.float32)
        for j in range(tiles):
            prepare(j)
            column = dot3(ah, al, bh[:, span(j)], bl[:, span(j)])
            raw[:, span(j)] = column
            total += squares(column)
        lane = lax.broadcasted_iota(jnp.int32, (8, 128), 1)
        sums_ref[...] = jnp.where(lane == 0, jnp.sum(total), grad_sum_ref[...])

    @pl.when(side == 0)
    def _():
        multiply(yh[:half], yl[:half], ph, pw, lambda j: unpack_column(pack, tiles, j, ph, pw))

    @pl.when(side != 0)
    def _():
        unpack_left(place_ref, pack, tiles, (0, tiles), lh, ll)
        multiply(lh[...], ll[...], yh, yl, lambda j: None)


def last_part(place, grad_sum, y_high, y_low, pack):
    size = y_high.shape[0]
    half = size // 2
    wide = pltpu.VMEM((half, size), jnp.bfloat16)
    big = pltpu.VMEM((size, size), jnp.bfloat16)
    return pl.pallas_call(
        last_kernel,
        out_shape=[
            pltpu.VMEM((half, size), jnp.float32),
            jax.ShapeDtypeStruct((8, 128), jnp.float32),
        ],
        in_specs=[smem()] + [vmem()] * 4,
        out_specs=[vmem(), vmem()],
        scratch_shapes=[big, big, wide, wide],
        compiler_params=pltpu.CompilerParams(vmem_limit_bytes=32 * MIB),
        cost_estimate=pl.CostEstimate(
            flops=3 * size**3, bytes_accessed=12 * 2**20, transcendentals=0
        ),
        name="last_part",
    )(place, grad_sum, resident(y_high), resident(y_low), resident(pack))


def graft_kernel(own_ref, other_ref, raw, out_hbm, buffer, sems):
    half, size = buffer.shape
    steps = sems.shape[0]
    count = size * size
    own = own_ref[...]
    raw_sum = own[:1, :1] + other_ref[:1, :1]
    grad_sum = own[:1, 1:2]
    scale = jnp.sqrt(grad_sum / count + epsilon) / jnp.sqrt(raw_sum / count + epsilon)
    stores = []
    for k in range(steps):
        rows = slice(k * half // steps, (k + 1) * half // steps)
        buffer[rows] = raw[rows] * scale
        stores.append(pltpu.make_async_copy(buffer.at[rows], out_hbm.at[rows], sems.at[k]))
        stores[-1].start()
    for store in stores:
        store.wait()


def graft(own_sums, other_sums, raw):
    steps = 4
    return pl.pallas_call(
        graft_kernel,
        out_shape=pltpu.HBM(raw.shape, jnp.float32),
        in_specs=[vmem(), vmem(), vmem()],
        out_specs=anywhere(),
        scratch_shapes=[
            pltpu.VMEM(raw.shape, jnp.float32),
            pltpu.SemaphoreType.DMA((steps,)),
        ],
        compiler_params=pltpu.CompilerParams(vmem_limit_bytes=6 * MIB),
        cost_estimate=pl.CostEstimate(flops=0, bytes_accessed=4 * 2**20, transcendentals=0),
        name="graft",
    )(own_sums, other_sums, resident(raw))


def renew_kernel(place_ref, a_ref, nh_ref, nl_ref, far_ref, out_ref, high_ref, low_ref):
    size = a_ref.shape[0]
    half = size // 2
    tiles = size // TILE
    side = place_ref[0]
    used = place_ref[1 + tiles] != 0

    for p in range(tiles):
        for c in range(tiles):
            if p < half // TILE:
                high, low = nh_ref[span(p), span(c)], nl_ref[span(p), span(c)]
            else:
                high, low = split(far_ref[span(p - half // TILE), span(c)])
            for block, target in ((high, high_ref), (low, low_ref)):
                target[side, span(p), span(c)] = block
                target[1 - side, span(c), span(p)] = block.T

    def write(i, j, block):
        i, j = (jnp.where(side == 0, place_ref[1 + k], k) for k in (i, j))
        rows = pl.ds(pl.multiple_of(i * TILE, TILE), TILE)
        cols = pl.ds(pl.multiple_of(j * TILE, TILE), TILE)
        gain = jnp.where(used, block * ((1.0 - decay_rate) / size), 0.0)
        out_ref[rows, cols] = decay_rate * a_ref[rows, cols] + gain

    for j in range(tiles):
        low_rows = slice(j * TILE, size)
        column = dot3(
            high_ref[0, low_rows, :], low_ref[0, low_rows, :],
            high_ref[1, :, span(j)], low_ref[1, :, span(j)],
        )
        for i in range(j, tiles):
            block = column[span(i - j)]
            write(i, j, block)
            if i != j:
                write(j, i, block.T)


def renew(place, factor, near_high, near_low, far):
    size = factor.shape[0]
    return pl.pallas_call(
        renew_kernel,
        out_shape=jax.ShapeDtypeStruct((size, size), jnp.float32),
        in_specs=[smem()] + [vmem()] * 4,
        out_specs=vmem(),
        scratch_shapes=[pltpu.VMEM((2, size, size), jnp.bfloat16)] * 2,
        compiler_params=pltpu.CompilerParams(vmem_limit_bytes=56 * MIB),
        cost_estimate=pl.CostEstimate(
            flops=4 * size**3, bytes_accessed=12 * 2**20, transcendentals=0
        ),
        name="renew",
    )(place, factor, near_high, near_low, far)


def per_device(grad, factors, owners):
    row_count = grad.shape[0]
    block_size = factors.shape[-1]
    owner_count = lax.axis_size("block")
    dp_index = lax.axis_index("dp")
    blk_index = lax.axis_index("block")
    side = dp_index % 2
    slot = dp_index // 2
    outer_pair = (dp_index == 0) | (dp_index == 3)
    groups = [
        [x * owner_count + b for x in pair for b in range(owner_count)] for pair in ((0, 3), (1, 2))
    ]

    def exchange(x):
        return lax.all_to_all(
            x, BOTH, split_axis=0, concat_axis=0, tiled=True, axis_index_groups=groups
        )

    def swap(x):
        return lax.ppermute(x, "dp", [(i, i ^ 1) for i in range(4)])

    order = jnp.where(outer_pair, jnp.array(OUTER_ORDER), jnp.array(INNER_ORDER))
    used = jnp.sum(owners == blk_index) > slot
    place = jnp.concatenate([side[None], order, used[None]]).astype(jnp.int32)

    near = exchange(deal(owners, grad, owner_count, False)).reshape(block_size // 2, block_size)
    other_grad = swap(grad)
    own_factor = factors[0, 0]
    x_high, x_low, pack = root(own_factor)
    pack, other_grad = lax.optimization_barrier((pack, other_grad))
    other_pack = swap(pack)
    dealt = deal(owners, other_grad, owner_count, True)
    near, dealt = lax.optimization_barrier((near, dealt))
    far = exchange(dealt).reshape(block_size // 2, block_size)

    early, near_high, near_low, near_sum = early_part(place, near, x_high, x_low)
    y_high, y_low, grad_sum = middle_part(place, near_sum, far, early, pack)
    raw, sums = last_part(place, grad_sum, y_high, y_low, other_pack)
    scaled = graft(sums, swap(sums), raw)
    scaled, far = lax.optimization_barrier((scaled, far))
    back = exchange(scaled.reshape(2 * owner_count, row_count, block_size))
    update = collect(owners, back)
    new_own = renew(place, own_factor, near_high, near_low, far)
    return (new_own[None, None], update)


def solution(mesh):
    placed = (P(BOTH, None), P("dp", "block", None, None), P())
    return jax.shard_map(
        per_device,
        mesh=mesh,
        in_specs=placed,
        out_specs=(P("dp", "block", None, None), P(BOTH, None)),
        check_vma=False,
    )
```
